32 devices in a mesh: aux: 2 (over x), ao: 4 (over y, core), orb: 4 (over z).
Axes of the slice: x: 2, y: 2, z: 4, core: 2. Of those that a mesh axis runs over, the one named last changes fastest.
Arguments:
- integrals: bfloat16 [32, 4, 4, 128, 128], P('aux', 'ao', None, 'orb'), may hold values from -6 to 6
- partner: int32 [4, 4], P('ao'), may hold values from 0 to 3
- pair_count: int32 [4], P('ao'), may hold values from 1 to 4
- occupied_coeff: bfloat16 [512, 512], P('ao', 'orb'), may hold values from -0.25 to 0.25
- occupied_domain: int32 [4, 4], P('ao', 'orb'), may hold values 0 or 1
- virtual_coeff: bfloat16 [512, 2048], P('aux', 'ao'), may hold values from -0.25 to 0.25
- virtual_domain: int32 [4, 16], P(None, 'ao'), may hold values 0 or 1
Outputs:
- transformed: bfloat16 [32, 512, 2048], P('aux', 'orb', 'ao')
The draws below stay inside these ranges and needn't reach their ends.
All inputs are finite; a program needn't handle non-finite values. No bound on the sum of `occupied_domain` or of `virtual_domain` on one device may be relied on, other than what follows from the above.
Results may differ from the reference program's by a relative error of at most 0.0049.
Values may be sent and summed in bfloat16 or wider, within the bound.
No kernel may reach another device: no remote copies, remote signals or barrier semaphores. Data moves between devices by JAX's collectives and lax.ppermute only.
A program may use at most 64 MiB of HBM per device.

```python
import jax
import jax.numpy as jnp
from jax import lax

BLK = 128
K = 4
AUX = 32
NBLK = 4
NAO = 512
NOCC = 512
NVIR = 2048
NOCB = 4
NVB = 16


def place_ends(drawn, stream_key, low, high):
    index_at = [jax.random.randint(jax.random.fold_in(stream_key, axis), (), 0, length) for axis, length in enumerate(drawn.shape)]
    main_axis = drawn.shape.index(max(drawn.shape))
    neighbour = index_at[:main_axis] + [(index_at[main_axis] + 1) % drawn.shape[main_axis]] + index_at[main_axis + 1:]
    return drawn.at[tuple(index_at)].set(low).at[tuple(neighbour)].set(high)


def shard_levels(own_key, shape, shards, least, high):
    def one(position, blocks):
        draws = jax.random.uniform(jax.random.fold_in(jax.random.fold_in(own_key, 6), position), (blocks,), jnp.float32, least / len(shards), high / len(shards))
        return jnp.repeat(jnp.exp(draws), shape[position] // blocks).reshape((-1,) + (1,) * (len(shape) - position - 1))

    factor_of = one(*shards[0])
    for cut in shards[1:]:
        factor_of = factor_of * one(*cut)
    return factor_of


def noise(stream_key, extent, spread, limit, split=(), kind=jnp.bfloat16):
    entries = spread * jax.random.normal(stream_key, extent, jnp.float32)
    if split:
        entries = entries * shard_levels(stream_key, extent, split, -0.22, 0.18)
    return jnp.clip(entries, -limit, limit).astype(kind)


def setup_inputs(seed: int = 0) -> dict:
    seeds = jax.random.split(jax.random.key(seed), 8)
    integrals = noise(seeds[0], (AUX, NBLK, K, BLK, BLK), 1.0, 6.0, ((0, 2), (1, 4), (3, 4)))
    partner = place_ends(jax.random.randint(seeds[1], (NBLK, K), 0, NBLK), jax.random.fold_in(seeds[1], 1), 0, NBLK - 1).astype(jnp.int32)
    pair_count = place_ends(jax.random.randint(seeds[2], (NBLK,), 1, K + 1), jax.random.fold_in(seeds[2], 1), 1, K).astype(jnp.int32)
    occupied_coeff = noise(seeds[3], (NAO, NOCC), (K * BLK) ** -0.5, 0.25, ((0, 4), (1, 4)))
    occupied_domain = place_ends((jax.random.randint(seeds[4], (NBLK, NOCB), 0, 4) < 3).astype(jnp.int32), jax.random.fold_in(seeds[4], 1), 0, 1)
    virtual_coeff = noise(seeds[5], (NAO, NVIR), NAO ** -0.5, 0.25, ((0, 2), (1, 4)))
    virtual_domain = place_ends((jax.random.randint(seeds[6], (NBLK, NVB), 0, 4) < 3).astype(jnp.int32), jax.random.fold_in(seeds[6], 1), 0, 1)
    return dict(integrals=integrals, partner=partner, pair_count=pair_count, occupied_coeff=occupied_coeff, occupied_domain=occupied_domain, virtual_coeff=virtual_coeff, virtual_domain=virtual_domain)


def reference(integrals, partner, pair_count, occupied_coeff, occupied_domain, virtual_coeff, virtual_domain):
    occ_mask = jnp.repeat(jnp.repeat(occupied_domain, BLK, axis=0), BLK, axis=1).astype(jnp.bfloat16)
    occupied_masked = occupied_coeff * occ_mask
    vir_mask = jnp.repeat(jnp.repeat(virtual_domain, BLK, axis=0), BLK, axis=1).astype(jnp.bfloat16)
    virtual_masked = virtual_coeff * vir_mask
    blocks = occupied_masked.reshape(NBLK, BLK, NOCC)[partner]
    slots = jnp.arange(K, dtype=jnp.int32)
    live = (slots[None, :] < pair_count[:, None]).astype(jnp.float32)
    blocks_wide = blocks.astype(jnp.float32) * live[:, :, None, None]

    def one_row(slab):
        half = jnp.einsum('nkri,nkrv->inv', blocks_wide, slab.astype(jnp.float32))
        half = half.reshape(NOCC, NAO).astype(jnp.bfloat16)
        return jnp.dot(half, virtual_masked, preferred_element_type=jnp.float32).astype(jnp.bfloat16)

    return lax.map(one_row, integrals)
```

```python
import functools

import jax
import jax.numpy as jnp
from jax import lax
from jax.experimental import pallas as pl
from jax.experimental.pallas import tpu as pltpu
from jax.sharding import PartitionSpec as P

BF16 = jnp.bfloat16
F32 = jnp.float32
VMEM_LIMIT = 48 * 1024 * 1024


def swap(x, axis, size, distance):
    return lax.ppermute(x, axis, [(i, i ^ distance) for i in range(size)])


def vmem():
    return pl.BlockSpec(memory_space=pltpu.VMEM)


def smem():
    return pl.BlockSpec(memory_space=pltpu.SMEM)


def half_kernel(orb_count, ao_count, scalars, *refs):
    raw = refs[:orb_count]
    occ = refs[orb_count : orb_count + ao_count]
    outs = refs[orb_count + ao_count : 2 * orb_count + ao_count]
    occ_all, left = refs[2 * orb_count + ao_count :]
    slabs, slots, rows, width = raw[0].shape
    block = occ[0].shape[1]
    for t in range(ao_count):
        occ_all[t] = occ[t][...]
    orb = scalars[2 * slots]
    for s in range(orb_count):
        start = pl.multiple_of((orb ^ s) * rows, rows)
        for k in range(slots):
            live = (scalars[slots + k]).astype(F32).astype(BF16)
            to = (s * slots + k) * rows
            for j in range(orb_count):
                part = occ_all[scalars[k], j, pl.ds(start, rows), :]
                left[to : to + rows, j * block : (j + 1) * block] = part * live
    right = jnp.concatenate(
        [
            jnp.concatenate(
                [raw[s][p].reshape(slots * rows, width) for s in range(orb_count)], axis=0
            )
            for p in range(slabs)
        ],
        axis=1,
    )
    wide = lax.dot_general(
        left[...], right, (((0,), (0,)), ((), ())), preferred_element_type=F32
    ).astype(BF16)
    for j in range(orb_count):
        for p in range(slabs):
            outs[j][p] = wide[j * block : (j + 1) * block, p * width : (p + 1) * width]


def virtual_kernel(aux_count, per_shard, scalars, domain, *refs):
    shards, out = refs[:aux_count], refs[aux_count]
    block = out.shape[1]
    for s in range(aux_count):
        for b in range(per_shard):
            n = (scalars[0] ^ s) * per_shard + b
            t = n ^ scalars[1]
            for c in range(out.shape[2] // block):
                mask = domain[n, c].astype(F32).astype(BF16)
                out[t, :, c * block : (c + 1) * block] = (
                    shards[s][b * block : (b + 1) * block, c * block : (c + 1) * block] * mask
                )


def final_kernel(ao_count, has_base, place, *refs):
    halves = refs[:ao_count]
    virtual = refs[ao_count]
    out = refs[-1]
    slabs, rows, block = halves[0].shape
    left = jnp.concatenate([h[...].reshape(slabs * rows, block) for h in halves], axis=1)
    right = virtual[...].reshape(ao_count * block, virtual.shape[2])
    wide = jnp.dot(left, right, preferred_element_type=F32)
    out[...] = wide.astype(out.dtype).reshape(out.shape)


def local(
    sizes, integrals, partner, pair_count, occupied_coeff, occupied_domain, virtual_coeff, virtual_domain
):
    aux_count, ao_count, orb_count = sizes
    chips = ao_count // 2
    aux, ao, orb = (lax.axis_index(name) for name in ("aux", "ao", "orb"))
    slab_rows, _, slots, rows, width = integrals.shape
    block = occupied_coeff.shape[0]
    share = slab_rows // orb_count
    raw_all = integrals.reshape(slab_rows, slots, rows, width)

    occ_own = occupied_coeff * occupied_domain[0, 0].astype(BF16)
    occ_orb = [occ_own] + [swap(occ_own, "orb", orb_count, s) for s in range(1, orb_count)]

    def raw_piece(s):
        return lax.dynamic_slice_in_dim(raw_all, (orb ^ s) * share, share, 0)

    raw = [raw_piece(0)] + [
        swap(raw_piece(s), "orb", orb_count, s) for s in range(1, orb_count)
    ]

    vir = [virtual_coeff] + [swap(virtual_coeff, "aux", aux_count, s) for s in range(1, aux_count)]

    occ_stack = jnp.stack(occ_orb)
    occ_chip = [occ_stack] + [swap(occ_stack, "ao", ao_count, 2 * t) for t in range(1, chips)]
    occ = []
    for piece in occ_chip:
        occ += [piece, swap(piece, "ao", ao_count, 1)]

    scalars = jnp.concatenate(
        [
            partner[0] ^ ao,
            (jnp.arange(slots, dtype=jnp.int32) < pair_count[0]).astype(jnp.int32),
            orb.astype(jnp.int32)[None],
        ]
    )
    halves = pl.pallas_call(
        functools.partial(half_kernel, orb_count, ao_count),
        out_shape=[jax.ShapeDtypeStruct((share, block, width), BF16)] * orb_count,
        in_specs=[smem()] + [vmem()] * (orb_count + ao_count),
        out_specs=[vmem()] * orb_count,
        scratch_shapes=[
            pltpu.VMEM((ao_count, orb_count, block, block), BF16),
            pltpu.VMEM((orb_count * slots * rows, orb_count * block), BF16),
        ],
        compiler_params=pltpu.CompilerParams(vmem_limit_bytes=VMEM_LIMIT),
        cost_estimate=pl.CostEstimate(
            flops=2 * share * orb_count * orb_count * slots * rows * block * width,
            bytes_accessed=2 * 1024 * 1024,
            transcendentals=0,
        ),
    )(scalars, *raw, *occ)

    virtual_width = virtual_coeff.shape[1]
    virtual = pl.pallas_call(
        functools.partial(virtual_kernel, aux_count, ao_count // aux_count),
        out_shape=jax.ShapeDtypeStruct((ao_count, block, virtual_width), BF16),
        in_specs=[smem(), smem()] + [vmem()] * aux_count,
        out_specs=vmem(),
        compiler_params=pltpu.CompilerParams(vmem_limit_bytes=VMEM_LIMIT),
        cost_estimate=pl.CostEstimate(
            flops=ao_count * block * virtual_width,
            bytes_accessed=4 * ao_count * block * virtual_width,
            transcendentals=0,
        ),
    )(jnp.stack([aux, ao]).astype(jnp.int32), virtual_domain, *vir)

    out_shape = jax.ShapeDtypeStruct((slab_rows, block, virtual_width), BF16)
    result = None
    for s in range(orb_count):
        mine = halves[s] if s == 0 else swap(halves[s], "orb", orb_count, s)
        over_chips = [mine] + [swap(mine, "ao", ao_count, 2 * t) for t in range(1, chips)]
        pieces = []
        for piece in over_chips:
            pieces += [piece, swap(piece, "ao", ao_count, 1)]
        place = (orb ^ s).astype(jnp.int32)[None]
        base = [] if result is None else [result]
        result = pl.pallas_call(
            functools.partial(final_kernel, ao_count, bool(base)),
            out_shape=out_shape,
            grid_spec=pltpu.PrefetchScalarGridSpec(
                num_scalar_prefetch=1,
                grid=(2,),
                in_specs=[
                    pl.BlockSpec((share // 2, block, width), lambda g, at: (g, 0, 0))
                ] * ao_count
                + [pl.BlockSpec((ao_count, block, virtual_width), lambda g, at: (0, 0, 0))]
                + [pl.BlockSpec(memory_space=pl.ANY)] * len(base),
                out_specs=pl.BlockSpec(
                    (share // 2, block, virtual_width), lambda g, at: (at[0] * 2 + g, 0, 0)
                ),
            ),
            input_output_aliases={ao_count + 2: 0} if base else {},
            compiler_params=pltpu.CompilerParams(vmem_limit_bytes=VMEM_LIMIT),
            cost_estimate=pl.CostEstimate(
                flops=2 * share * block * ao_count * block * virtual_width,
                bytes_accessed=2 * 1024 * 1024,
                transcendentals=0,
            ),
        )(place, *pieces, virtual, *base)
    return result


def solution(mesh):
    placed = (
        P("aux", "ao", None, "orb", None),
        P("ao", None),
        P("ao"),
        P("ao", "orb"),
        P("ao", "orb"),
        P("aux", "ao"),
        P(None, "ao"),
    )
    sizes = tuple(mesh.shape[name] for name in ("aux", "ao", "orb"))
    return jax.shard_map(
        functools.partial(local, sizes),
        mesh=mesh,
        in_specs=placed,
        out_specs=P("aux", "orb", "ao"),
        check_vma=False,
    )
```

```python
import functools

import jax
import jax.numpy as jnp
from jax import lax
from jax.experimental import pallas as pl
from jax.experimental.pallas import tpu as pltpu
from jax.sharding import PartitionSpec as P

BF16 = jnp.bfloat16
F32 = jnp.float32
VMEM_LIMIT = 48 * 1024 * 1024


def swap(x, axis, size, distance):
    return lax.ppermute(x, axis, [(i, i ^ distance) for i in range(size)])


def vmem():
    return pl.BlockSpec(memory_space=pltpu.VMEM)


def smem():
    return pl.BlockSpec(memory_space=pltpu.SMEM)


def anywhere():
    return pl.BlockSpec(memory_space=pl.ANY)


def as_bf16(value):
    return value.astype(F32).astype(BF16)


def call(body, flops, touched, **rest):
    return pl.pallas_call(
        body,
        compiler_params=pltpu.CompilerParams(vmem_limit_bytes=VMEM_LIMIT),
        cost_estimate=pl.CostEstimate(
            flops=flops, bytes_accessed=touched, transcendentals=0
        ),
        **rest,
    )


def slice_kernel(distances, with_occ, orb, *refs):
    sems = refs[-1]
    raw = refs[0]
    refs = refs[1:]
    if with_occ:
        domain, coeff = refs[:2]
        refs = refs[2:]
    outs = refs[: len(distances)]
    share = outs[0].shape[0]
    copies = [
        pltpu.make_async_copy(
            raw.at[pl.ds((orb[0] ^ s) * share, share)], outs[w], sems.at[w]
        )
        for w, s in enumerate(distances)
    ]
    for copy in copies:
        copy.start()
    if with_occ:
        refs[len(distances)][...] = coeff[...] * as_bf16(domain[0, 0])
    for copy in copies:
        copy.wait()


def half_kernel(orb_count, ao_count, wanted, extra, orb, ao, partner, pair_count, *refs):
    raw = refs[:orb_count]
    occ = refs[orb_count : orb_count + ao_count]
    at = orb_count + ao_count + extra
    outs = refs[at : at + len(wanted)]
    left = refs[at + len(wanted)]
    slabs, slots, rows, width = raw[0].shape
    block = occ[0].shape[1]
    occ_all = refs[at + len(wanted) + 1]
    for t in range(ao_count):
        for w, j in enumerate(wanted):
            occ_all[t, w] = occ[t][j]
    for k in range(slots):
        live = as_bf16((k < pair_count[0]).astype(jnp.int32))
        source = partner[0, k] ^ ao[0]
        for s in range(orb_count):
            start = pl.multiple_of((orb[0] ^ s) * rows, rows)
            to = (s * slots + k) * rows
            for w in range(len(wanted)):
                left[to : to + rows, w * block : (w + 1) * block] = (
                    occ_all[source, w, pl.ds(start, rows), :] * live
                )
    right = jnp.concatenate(
        [
            jnp.concatenate(
                [raw[s][p].reshape(slots * rows, width) for s in range(orb_count)], axis=0
            )
            for p in range(slabs)
        ],
        axis=1,
    )
    wide = lax.dot_general(
        left[...], right, (((0,), (0,)), ((), ())), preferred_element_type=F32
    ).astype(BF16)
    for w in range(len(wanted)):
        for p in range(slabs):
            outs[w][p] = wide[w * block : (w + 1) * block, p * width : (p + 1) * width]


def virtual_kernel(aux_count, per_shard, aux, ao, domain, *refs):
    shards, out = refs[:aux_count], refs[aux_count]
    block = out.shape[1]
    for s in range(aux_count):
        for b in range(per_shard):
            n = (aux[0] ^ s) * per_shard + b
            t = n ^ ao[0]
            for c in range(out.shape[2] // block):
                out[t, :, c * block : (c + 1) * block] = shards[s][
                    b * block : (b + 1) * block, c * block : (c + 1) * block
                ] * as_bf16(domain[n, c])


def final_kernel(ao_count, place, *refs):
    halves = refs[:ao_count]
    virtual = refs[ao_count]
    out = refs[-1]
    slabs, rows, block = halves[0].shape
    left = jnp.concatenate([h[...].reshape(slabs * rows, block) for h in halves], axis=1)
    right = virtual[...].reshape(ao_count * block, virtual.shape[2])
    wide = jnp.dot(left, right, preferred_element_type=F32)
    out[...] = wide.astype(out.dtype).reshape(out.shape)


def local(
    sizes, integrals, partner, pair_count, occupied_coeff, occupied_domain, virtual_coeff, virtual_domain
):
    aux_count, ao_count, orb_count = sizes
    chips = ao_count // 2
    aux, ao, orb = (
        lax.axis_index(name).astype(jnp.int32)[None] for name in ("aux", "ao", "orb")
    )
    slab_rows, _, slots, rows, width = integrals.shape
    block = occupied_coeff.shape[0]
    share = slab_rows // orb_count
    raw_all = integrals.reshape(slab_rows, slots, rows, width)
    far = [s for s in range(orb_count) if s >= orb_count // 2]
    near = [s for s in range(orb_count) if s < orb_count // 2]

    piece = jax.ShapeDtypeStruct((share, slots, rows, width), BF16)
    raw = {}
    made = call(
        functools.partial(slice_kernel, far, True),
        occupied_coeff.size,
        len(far) * 2 * share * slots * rows * width * 2,
        out_shape=[piece] * len(far) + [jax.ShapeDtypeStruct(occupied_coeff.shape, BF16)],
        in_specs=[smem(), anywhere(), smem(), vmem()],
        out_specs=[vmem()] * (len(far) + 1),
        scratch_shapes=[pltpu.SemaphoreType.DMA((len(far),))],
    )(orb, raw_all, occupied_domain, occupied_coeff)
    occ_own = made[-1]
    for s, sent in zip(far, made):
        raw[s] = swap(sent, "orb", orb_count, s)
    made = call(
        functools.partial(slice_kernel, near, False),
        0,
        len(near) * 2 * share * slots * rows * width * 2,
        out_shape=[piece] * len(near),
        in_specs=[smem(), anywhere()],
        out_specs=[vmem()] * len(near),
        scratch_shapes=[pltpu.SemaphoreType.DMA((len(near),))],
    )(orb, raw_all)
    for s, sent in zip(near, made):
        raw[s] = swap(sent, "orb", orb_count, s) if s else sent

    occ_orb = [occ_own] + [swap(occ_own, "orb", orb_count, s) for s in range(1, orb_count)]
    occ_stack = jnp.stack(occ_orb)
    occ_chip = [occ_stack] + [swap(occ_stack, "ao", ao_count, 2 * t) for t in range(1, chips)]
    occ = []
    for part in occ_chip:
        occ += [part, swap(part, "ao", ao_count, 1)]

    vir = [virtual_coeff] + [swap(virtual_coeff, "aux", aux_count, s) for s in range(1, aux_count)]
    virtual_width = virtual_coeff.shape[1]
    virtual = call(
        functools.partial(virtual_kernel, aux_count, ao_count // aux_count),
        ao_count * block * virtual_width,
        4 * ao_count * block * virtual_width,
        out_shape=jax.ShapeDtypeStruct((ao_count, block, virtual_width), BF16),
        in_specs=[smem()] * 3 + [vmem()] * aux_count,
        out_specs=vmem(),
    )(aux, ao, virtual_domain, *vir)

    def half(wanted, *after):
        return call(
            functools.partial(half_kernel, orb_count, ao_count, wanted, len(after)),
            2 * share * orb_count * len(wanted) * slots * rows * block * width,
            1024 * 1024,
            out_shape=[jax.ShapeDtypeStruct((share, block, width), BF16)] * len(wanted),
            in_specs=[smem()] * 4 + [vmem()] * (orb_count + ao_count) + [anywhere()] * len(after),
            out_specs=[vmem()] * len(wanted),
            scratch_shapes=[
                pltpu.VMEM((orb_count * slots * rows, len(wanted) * block), BF16),
                pltpu.VMEM((ao_count, len(wanted), block, block), BF16),
            ],
        )(orb, ao, partner, pair_count, *(raw[s] for s in range(orb_count)), *occ, *after)

    mine = {}
    order = [far[0]] + near[::-1] + far[1:]
    (sent,) = half(order[:1])
    mine[order[0]] = swap(sent, "orb", orb_count, order[0])
    made = half(near[::-1], sent)
    for s, sent in zip(near[::-1], made):
        mine[s] = swap(sent, "orb", orb_count, s) if s else sent
    for s in far[1:]:
        (sent,) = half([s], mine[near[-1]])
        mine[s] = swap(sent, "orb", orb_count, s)

    result = None
    for s in near + far:
        over_chips = [mine[s]] + [swap(mine[s], "ao", ao_count, 2 * t) for t in range(1, chips)]
        pieces = []
        for part in over_chips:
            pieces += [part, swap(part, "ao", ao_count, 1)]
        base = [] if result is None else [result]
        result = call(
            functools.partial(final_kernel, ao_count),
            20 * share * block * ao_count * block * virtual_width,
            20 * 1024 * 1024,
            out_shape=jax.ShapeDtypeStruct((slab_rows, block, virtual_width), BF16),
            grid_spec=pltpu.PrefetchScalarGridSpec(
                num_scalar_prefetch=1,
                grid=(2,),
                in_specs=[pl.BlockSpec((share // 2, block, width), lambda g, at: (g, 0, 0))]
                * ao_count
                + [pl.BlockSpec((ao_count, block, virtual_width), lambda g, at: (0, 0, 0))]
                + [anywhere()] * len(base),
                out_specs=pl.BlockSpec(
                    (share // 2, block, virtual_width), lambda g, at: (at[0] * 2 + g, 0, 0)
                ),
            ),
            input_output_aliases={ao_count + 2: 0} if base else {},
        )(orb ^ s, *pieces, virtual, *base)
    return result


def solution(mesh):
    placed = (
        P("aux", "ao", None, "orb", None),
        P("ao", None),
        P("ao"),
        P("ao", "orb"),
        P("ao", "orb"),
        P("aux", "ao"),
        P(None, "ao"),
    )
    sizes = tuple(mesh.shape[name] for name in ("aux", "ao", "orb"))
    return jax.shard_map(
        functools.partial(local, sizes),
        mesh=mesh,
        in_specs=placed,
        out_specs=P("aux", "orb", "ao"),
        check_vma=False,
    )
```

```python
import functools

import jax
import jax.numpy as jnp
from jax import lax
from jax.experimental import pallas as pl
from jax.experimental.pallas import tpu as pltpu
from jax.sharding import PartitionSpec as P

BF16 = jnp.bfloat16
F32 = jnp.float32
VMEM_LIMIT = 48 * 1024 * 1024
CHUNKS = 2


def swap(x, axis, size, distance):
    return lax.ppermute(x, axis, [(i, i ^ distance) for i in range(size)])


def vmem():
    return pl.BlockSpec(memory_space=pltpu.VMEM)


def smem():
    return pl.BlockSpec(memory_space=pltpu.SMEM)


def anywhere():
    return pl.BlockSpec(memory_space=pl.ANY)


def as_bf16(value):
    return value.astype(F32).astype(BF16)


def call(body, flops, touched, **rest):
    return pl.pallas_call(
        body,
        compiler_params=pltpu.CompilerParams(vmem_limit_bytes=VMEM_LIMIT),
        cost_estimate=pl.CostEstimate(
            flops=flops, bytes_accessed=touched, transcendentals=0
        ),
        **rest,
    )


def slice_kernel(orb, domain, raw, coeff, *refs):
    sent, kept, own, sems = refs[:CHUNKS], refs[CHUNKS : 2 * CHUNKS], refs[-2], refs[-1]
    rows = kept[0].shape[0]
    half = orb[0] // 2
    copies = []
    for c in range(CHUNKS):
        for w, (where, to) in enumerate(((1 - half, sent[c]), (half, kept[c]))):
            start = pl.multiple_of((where * CHUNKS + c) * rows, rows)
            copies.append(
                pltpu.make_async_copy(
                    raw.at[pl.ds(start, rows)], to.at[pl.ds(0, rows)], sems.at[2 * c + w]
                )
            )
    for copy in copies:
        copy.start()
    masked = coeff[...] * as_bf16(domain[0, 0])
    own[...] = masked
    sent[0][rows:, :] = masked
    for copy in copies:
        copy.wait()


def split_kernel(own, message, raw, pair):
    rows = raw.shape[0]
    raw[...] = message[:rows]
    pair[0] = own[...]
    pair[1] = message[rows:]


def left_kernel(ao_count, slots, rows, orb, ao, partner, pair_count, *refs):
    occ, out, occ_all, upright = refs[:ao_count], refs[-3], refs[-2], refs[-1]
    blocks, block, _ = occ[0].shape
    for t in range(ao_count):
        occ_all[t] = occ[t][...]
    for k in range(slots):
        live = as_bf16((k < pair_count[0]).astype(jnp.int32))
        source = partner[0, k] ^ ao[0]
        for s in range(block // rows):
            start = pl.multiple_of((orb[0] ^ s) * rows, rows)
            to = (s * slots + k) * rows
            for w in range(blocks):
                upright[to : to + rows, w * block : (w + 1) * block] = (
                    occ_all[source, w, pl.ds(start, rows), :] * live
                )
    out[...] = upright[...].T


def half_kernel(slot_rows, left, *refs):
    raw, outs = refs[:4], refs[4:]
    slabs, block, width = outs[0].shape
    right = jnp.concatenate(
        [
            jnp.concatenate(
                [part[p * slot_rows : (p + 1) * slot_rows, :] for part in raw], axis=0
            )
            for p in range(slabs)
        ],
        axis=1,
    )
    wide = jnp.dot(left[...], right, preferred_element_type=F32).astype(BF16)
    for w in range(len(outs)):
        for p in range(slabs):
            outs[w][p] = wide[w * block : (w + 1) * block, p * width : (p + 1) * width]


def virtual_kernel(aux_count, per_shard, aux, ao, domain, *refs):
    shards, out = refs[:aux_count], refs[aux_count]
    block = out.shape[1]
    for s in range(aux_count):
        for b in range(per_shard):
            n = (aux[0] ^ s) * per_shard + b
            t = n ^ ao[0]
            for c in range(out.shape[2] // block):
                out[t, :, c * block : (c + 1) * block] = shards[s][
                    b * block : (b + 1) * block, c * block : (c + 1) * block
                ] * as_bf16(domain[n, c])


def final_kernel(ao_count, place, *refs):
    halves = refs[:ao_count]
    virtual = refs[ao_count]
    out = refs[-1]
    slabs, rows, block = halves[0].shape
    left = jnp.concatenate([h[...].reshape(slabs * rows, block) for h in halves], axis=1)
    right = virtual[...].reshape(ao_count * block, virtual.shape[2])
    wide = jnp.dot(left, right, preferred_element_type=F32)
    out[...] = wide.astype(out.dtype).reshape(out.shape)


def local(
    sizes, integrals, partner, pair_count, occupied_coeff, occupied_domain, virtual_coeff, virtual_domain
):
    aux_count, ao_count, orb_count = sizes
    chips = ao_count // 2
    aux, ao, orb = (
        lax.axis_index(name).astype(jnp.int32)[None] for name in ("aux", "ao", "orb")
    )
    slab_rows, _, slots, rows, width = integrals.shape
    block = occupied_coeff.shape[0]
    share = slab_rows // (2 * CHUNKS)
    slot_rows = slots * rows
    piece_rows = share * slot_rows

    def array(*shape):
        return jax.ShapeDtypeStruct(shape, BF16)

    made = call(
        slice_kernel,
        block * block,
        2 * integrals.size * 2,
        out_shape=[array(piece_rows + block * (c == 0), width) for c in range(CHUNKS)]
        + [array(piece_rows, width)] * CHUNKS
        + [array(block, block)],
        in_specs=[smem(), smem(), anywhere(), vmem()],
        out_specs=[vmem()] * (2 * CHUNKS + 1),
        scratch_shapes=[pltpu.SemaphoreType.DMA((2 * CHUNKS,))],
    )(orb, occupied_domain, integrals.reshape(slab_rows * slot_rows, width), occupied_coeff)
    crossed = [swap(part, "orb", orb_count, 2) for part in made[:CHUNKS]]
    kept = made[CHUNKS : 2 * CHUNKS]
    crossed[0], occ_pair = call(
        split_kernel,
        block * block,
        4 * piece_rows * width,
        out_shape=[array(piece_rows, width), array(2, block, block)],
        in_specs=[vmem()] * 2,
        out_specs=[vmem()] * 2,
    )(made[-1], crossed[0])

    beside = [swap(part, "orb", orb_count, 1) for part in kept]
    across = [swap(part, "orb", orb_count, 1) for part in crossed]

    occ = []
    for part in [occ_pair] + [swap(occ_pair, "ao", ao_count, 2 * t) for t in range(1, chips)]:
        occ += [part, swap(part, "ao", ao_count, 1)]
    left = call(
        functools.partial(left_kernel, ao_count, slots, rows),
        2 * block * slots * block,
        8 * block * slots * block,
        out_shape=array(2 * block, slots * block),
        in_specs=[smem()] * 4 + [vmem()] * ao_count,
        out_specs=vmem(),
        scratch_shapes=[
            pltpu.VMEM((ao_count, 2, block, block), BF16),
            pltpu.VMEM((slots * block, 2 * block), BF16),
        ],
    )(orb, ao, partner, pair_count, *occ)

    vir = [virtual_coeff] + [swap(virtual_coeff, "aux", aux_count, s) for s in range(1, aux_count)]
    virtual_width = virtual_coeff.shape[1]
    virtual = call(
        functools.partial(virtual_kernel, aux_count, ao_count // aux_count),
        ao_count * block * virtual_width,
        4 * ao_count * block * virtual_width,
        out_shape=array(ao_count, block, virtual_width),
        in_specs=[smem()] * 3 + [vmem()] * aux_count,
        out_specs=vmem(),
    )(aux, ao, virtual_domain, *vir)

    parts = []
    for c in range(CHUNKS):
        own, sent = call(
            functools.partial(half_kernel, slot_rows),
            2 * share * 2 * block * slots * block * width,
            12 * piece_rows * width,
            out_shape=[array(share, block, width)] * 2,
            in_specs=[vmem()] * 5,
            out_specs=[vmem()] * 2,
        )(left, kept[c], beside[c], crossed[c], across[c])
        parts.append((orb // 2 * CHUNKS + c, own))
        parts.append(((1 - orb // 2) * CHUNKS + c, swap(sent, "orb", orb_count, 2)))

    result = None
    for place, mine in parts:
        pieces = []
        for part in [mine] + [swap(mine, "ao", ao_count, 2 * t) for t in range(1, chips)]:
            pieces += [part, swap(part, "ao", ao_count, 1)]
        base = [] if result is None else [result]
        result = call(
            functools.partial(final_kernel, ao_count),
            20 * share * block * ao_count * block * virtual_width,
            20 * 1024 * 1024,
            out_shape=array(slab_rows, block, virtual_width),
            grid_spec=pltpu.PrefetchScalarGridSpec(
                num_scalar_prefetch=1,
                grid=(2,),
                in_specs=[pl.BlockSpec((share // 2, block, width), lambda g, at: (g, 0, 0))]
                * ao_count
                + [pl.BlockSpec((ao_count, block, virtual_width), lambda g, at: (0, 0, 0))]
                + [anywhere()] * len(base),
                out_specs=pl.BlockSpec(
                    (share // 2, block, virtual_width), lambda g, at: (at[0] * 2 + g, 0, 0)
                ),
            ),
            input_output_aliases={ao_count + 2: 0} if base else {},
        )(place, *pieces, virtual, *base)
    return result


def solution(mesh):
    placed = (
        P("aux", "ao", None, "orb", None),
        P("ao", None),
        P("ao"),
        P("ao", "orb"),
        P("ao", "orb"),
        P("aux", "ao"),
        P(None, "ao"),
    )
    sizes = tuple(mesh.shape[name] for name in ("aux", "ao", "orb"))
    return jax.shard_map(
        functools.partial(local, sizes),
        mesh=mesh,
        in_specs=placed,
        out_specs=P("aux", "orb", "ao"),
        check_vma=False,
    )
```

```python
import functools

import jax
import jax.numpy as jnp
from jax import lax
from jax.experimental import pallas as pl
from jax.experimental.pallas import tpu as pltpu
from jax.sharding import PartitionSpec as P

BF16 = jnp.bfloat16
F32 = jnp.float32
VMEM_LIMIT = 48 * 1024 * 1024


def swap(x, axis, size, distance):
    return lax.ppermute(x, axis, [(i, i ^ distance) for i in range(size)])


def vmem():
    return pl.BlockSpec(memory_space=pltpu.VMEM)


def smem():
    return pl.BlockSpec(memory_space=pltpu.SMEM)


def stack_kernel(*refs):
    for j, part in enumerate(refs[:-1]):
        refs[-1][j] = part[...]


def half_kernel(orb_count, ao_count, scalars, *refs):
    raw = refs[:orb_count]
    occ = refs[orb_count : orb_count + ao_count]
    outs = refs[orb_count + ao_count : 2 * orb_count + ao_count]
    occ_all, left = refs[2 * orb_count + ao_count :]
    slabs, slots, rows, width = raw[0].shape
    block = occ[0].shape[1]
    for t in range(ao_count):
        occ_all[t] = occ[t][...]
    orb = scalars[2 * slots]
    for s in range(orb_count):
        start = pl.multiple_of((orb ^ s) * rows, rows)
        for k in range(slots):
            live = (scalars[slots + k]).astype(F32).astype(BF16)
            to = (s * slots + k) * rows
            for j in range(orb_count):
                part = occ_all[scalars[k], j, pl.ds(start, rows), :]
                left[to : to + rows, j * block : (j + 1) * block] = part * live
    right = jnp.concatenate(
        [
            jnp.concatenate(
                [raw[s][p].reshape(slots * rows, width) for s in range(orb_count)], axis=0
            )
            for p in range(slabs)
        ],
        axis=1,
    )
    wide = lax.dot_general(
        left[...], right, (((0,), (0,)), ((), ())), preferred_element_type=F32
    ).astype(BF16)
    for j in range(orb_count):
        for p in range(slabs):
            outs[j][p] = wide[j * block : (j + 1) * block, p * width : (p + 1) * width]


def virtual_kernel(aux_count, per_shard, scalars, domain, *refs):
    shards, out = refs[:aux_count], refs[aux_count]
    block = out.shape[1]
    for s in range(aux_count):
        for b in range(per_shard):
            n = (scalars[0] ^ s) * per_shard + b
            t = n ^ scalars[1]
            for c in range(out.shape[2] // block):
                mask = domain[n, c].astype(F32).astype(BF16)
                out[t, :, c * block : (c + 1) * block] = (
                    shards[s][b * block : (b + 1) * block, c * block : (c + 1) * block] * mask
                )


def final_kernel(ao_count, distances, orb, virtual, *refs):
    halves, out, made, sems = refs[: ao_count * len(distances)], refs[-3], refs[-2], refs[-1]
    slabs, rows, block = halves[0].shape
    right = virtual[...].reshape(ao_count * block, virtual.shape[2])
    copies = []
    for w, s in enumerate(distances):
        left = jnp.concatenate(
            [h[...].reshape(slabs * rows, block) for h in halves[w * ao_count : (w + 1) * ao_count]],
            axis=1,
        )
        wide = jnp.dot(left, right, preferred_element_type=F32)
        made[w] = wide.astype(made.dtype).reshape(made.shape[1:])
        start = pl.multiple_of((orb[0] ^ s) * slabs, slabs)
        copy = pltpu.make_async_copy(made.at[w], out.at[pl.ds(start, slabs)], sems.at[w])
        copy.start()
        copies.append(copy)
    for copy in copies:
        copy.wait()


def local(
    sizes, integrals, partner, pair_count, occupied_coeff, occupied_domain, virtual_coeff, virtual_domain
):
    aux_count, ao_count, orb_count = sizes
    chips = ao_count // 2
    aux, ao, orb = (lax.axis_index(name) for name in ("aux", "ao", "orb"))
    slab_rows, _, slots, rows, width = integrals.shape
    block = occupied_coeff.shape[0]
    share = slab_rows // orb_count
    order = [2, 3, 1, 0]
    raw_all = integrals.reshape(slab_rows, slots, rows, width)

    occ_own = occupied_coeff * occupied_domain[0, 0].astype(BF16)
    occ_by = {s: swap(occ_own, "orb", orb_count, s) if s else occ_own for s in order}
    occ_orb = [occ_by[s] for s in range(orb_count)]

    def raw_piece(s):
        return lax.dynamic_slice_in_dim(raw_all, (orb ^ s) * share, share, 0)

    raw_by = {s: swap(raw_piece(s), "orb", orb_count, s) if s else raw_piece(s) for s in order}
    raw = [raw_by[s] for s in range(orb_count)]

    vir = [virtual_coeff] + [swap(virtual_coeff, "aux", aux_count, s) for s in range(1, aux_count)]

    occ_stack = pl.pallas_call(
        stack_kernel,
        out_shape=jax.ShapeDtypeStruct((orb_count, block, block), BF16),
        in_specs=[vmem()] * orb_count,
        out_specs=vmem(),
    )(*occ_orb)
    occ_chip = [occ_stack] + [swap(occ_stack, "ao", ao_count, 2 * t) for t in range(1, chips)]
    occ = []
    for piece in occ_chip:
        occ += [piece, swap(piece, "ao", ao_count, 1)]

    scalars = jnp.concatenate(
        [
            partner[0] ^ ao,
            (jnp.arange(slots, dtype=jnp.int32) < pair_count[0]).astype(jnp.int32),
            orb.astype(jnp.int32)[None],
        ]
    )
    halves = pl.pallas_call(
        functools.partial(half_kernel, orb_count, ao_count),
        out_shape=[jax.ShapeDtypeStruct((share, block, width), BF16)] * orb_count,
        in_specs=[smem()] + [vmem()] * (orb_count + ao_count),
        out_specs=[vmem()] * orb_count,
        scratch_shapes=[
            pltpu.VMEM((ao_count, orb_count, block, block), BF16),
            pltpu.VMEM((orb_count * slots * rows, orb_count * block), BF16),
        ],
        compiler_params=pltpu.CompilerParams(vmem_limit_bytes=VMEM_LIMIT),
        cost_estimate=pl.CostEstimate(
            flops=2 * share * orb_count * orb_count * slots * rows * block * width,
            bytes_accessed=2 * 1024 * 1024,
            transcendentals=0,
        ),
    )(scalars, *raw, *occ)

    virtual_width = virtual_coeff.shape[1]
    virtual = pl.pallas_call(
        functools.partial(virtual_kernel, aux_count, ao_count // aux_count),
        out_shape=jax.ShapeDtypeStruct((ao_count, block, virtual_width), BF16),
        in_specs=[smem(), smem()] + [vmem()] * aux_count,
        out_specs=vmem(),
        compiler_params=pltpu.CompilerParams(vmem_limit_bytes=VMEM_LIMIT),
        cost_estimate=pl.CostEstimate(
            flops=ao_count * block * virtual_width,
            bytes_accessed=4 * ao_count * block * virtual_width,
            transcendentals=0,
        ),
    )(jnp.stack([aux, ao]).astype(jnp.int32), virtual_domain, *vir)

    pieces = {}
    for s in order:
        mine = swap(halves[s], "orb", orb_count, s) if s else halves[s]
        pieces[s] = []
        for part in [mine] + [swap(mine, "ao", ao_count, 2 * t) for t in range(1, chips)]:
            pieces[s] += [part, swap(part, "ao", ao_count, 1)]

    result = []
    for distances in [[0, 1], [2, 3]]:
        taken = [part for s in distances for part in pieces[s]]
        result = [
            pl.pallas_call(
                functools.partial(final_kernel, ao_count, distances),
                out_shape=jax.ShapeDtypeStruct((slab_rows, block, virtual_width), BF16),
                in_specs=[smem()] + [vmem()] * (1 + len(taken))
                + [pl.BlockSpec(memory_space=pl.ANY)] * len(result),
                out_specs=pl.BlockSpec(memory_space=pl.ANY),
                scratch_shapes=[
                    pltpu.VMEM((len(distances), share, block, virtual_width), BF16),
                    pltpu.SemaphoreType.DMA((len(distances),)),
                ],
                input_output_aliases={2 + len(taken): 0} if result else {},
                compiler_params=pltpu.CompilerParams(vmem_limit_bytes=VMEM_LIMIT),
                cost_estimate=pl.CostEstimate(
                    flops=2 * len(distances) * share * block * ao_count * block * virtual_width,
                    bytes_accessed=len(distances) * 2 * 1024 * 1024,
                    transcendentals=0,
                ),
            )(orb.astype(jnp.int32)[None], virtual, *taken, *result)
        ]
    return result[0]


def solution(mesh):
    placed = (
        P("aux", "ao", None, "orb", None),
        P("ao", None),
        P("ao"),
        P("ao", "orb"),
        P("ao", "orb"),
        P("aux", "ao"),
        P(None, "ao"),
    )
    sizes = tuple(mesh.shape[name] for name in ("aux", "ao", "orb"))
    return jax.shard_map(
        functools.partial(local, sizes),
        mesh=mesh,
        in_specs=placed,
        out_specs=P("aux", "orb", "ao"),
        check_vma=False,
    )
```

```python
import functools

import jax
import jax.numpy as jnp
from jax import lax
from jax.experimental import pallas as pl
from jax.experimental.pallas import tpu as pltpu
from jax.sharding import PartitionSpec as P

BF16 = jnp.bfloat16
F32 = jnp.float32
VMEM_LIMIT = 32 * 1024 * 1024


def swap(x, axis, size, distance):
    return lax.ppermute(x, axis, [(i, i ^ distance) for i in range(size)])


def vmem():
    return pl.BlockSpec(memory_space=pltpu.VMEM)


def smem():
    return pl.BlockSpec(memory_space=pltpu.SMEM)


def stack_kernel(*refs):
    for j, part in enumerate(refs[:-1]):
        refs[-1][j] = part[...]


def half_kernel(orb_count, ao_count, scalars, *refs):
    raw = refs[:orb_count]
    occ = refs[orb_count : orb_count + ao_count]
    outs = refs[orb_count + ao_count : 2 * orb_count + ao_count]
    occ_all, left = refs[2 * orb_count + ao_count :]
    slabs, slots, rows, width = raw[0].shape
    block = occ[0].shape[1]
    for t in range(ao_count):
        occ_all[t] = occ[t][...]
    orb = scalars[2 * slots]
    for s in range(orb_count):
        start = pl.multiple_of((orb ^ s) * rows, rows)
        for k in range(slots):
            live = (scalars[slots + k]).astype(F32).astype(BF16)
            to = (s * slots + k) * rows
            for j in range(orb_count):
                part = occ_all[scalars[k], j, pl.ds(start, rows), :]
                left[to : to + rows, j * block : (j + 1) * block] = part * live
    right = jnp.concatenate(
        [
            jnp.concatenate(
                [raw[s][p].reshape(slots * rows, width) for s in range(orb_count)], axis=0
            )
            for p in range(slabs)
        ],
        axis=1,
    )
    wide = lax.dot_general(
        left[...], right, (((0,), (0,)), ((), ())), preferred_element_type=F32
    ).astype(BF16)
    for j in range(orb_count):
        for p in range(slabs):
            outs[j][p] = wide[j * block : (j + 1) * block, p * width : (p + 1) * width]


def mask_kernel(per_shard, aux, domain, coeff, after, out):
    width = coeff.shape[1] // domain.shape[1]
    block = coeff.shape[0] // per_shard
    for b in range(per_shard):
        for c in range(domain.shape[1]):
            at = (slice(b * block, (b + 1) * block), slice(c * width, (c + 1) * width))
            mask = domain[aux[0] * per_shard + b, c].astype(F32).astype(BF16)
            out[at] = coeff[at] * mask


def virtual_kernel(aux_count, per_shard, aux, ao, *refs):
    shards, out = refs[:aux_count], refs[aux_count]
    block = out.shape[1]
    for s in range(aux_count):
        for b in range(per_shard):
            out[((aux[0] ^ s) * per_shard + b) ^ ao[0]] = shards[s][b * block : (b + 1) * block]


def final_kernel(ao_count, distances, orb, virtual, *refs):
    halves, (out, token, made, sems) = refs[: ao_count * len(distances)], refs[-4:]
    slabs, rows, block = halves[0].shape
    right = virtual[...].reshape(ao_count * block, virtual.shape[2])
    copies = []
    for w, s in enumerate(distances):
        left = jnp.concatenate(
            [h[...].reshape(slabs * rows, block) for h in halves[w * ao_count : (w + 1) * ao_count]],
            axis=1,
        )
        wide = jnp.dot(left, right, preferred_element_type=F32)
        made[w] = wide.astype(made.dtype).reshape(made.shape[1:])
        start = pl.multiple_of((orb[0] ^ s) * slabs, slabs)
        copy = pltpu.make_async_copy(made.at[w], out.at[pl.ds(start, slabs)], sems.at[w])
        copy.start()
        copies.append(copy)
    for copy in copies:
        copy.wait()
    token[...] = jnp.zeros_like(token)


def gate_kernel(part, after, out):
    out[...] = part[...]


def local(
    sizes, integrals, partner, pair_count, occupied_coeff, occupied_domain, virtual_coeff, virtual_domain
):
    aux_count, ao_count, orb_count = sizes
    chips = ao_count // 2
    aux, ao, orb = (lax.axis_index(name) for name in ("aux", "ao", "orb"))
    slab_rows, _, slots, rows, width = integrals.shape
    block = occupied_coeff.shape[0]
    share = slab_rows // orb_count
    order = [1, 2, 3, 0]
    raw_all = integrals.reshape(slab_rows, slots, rows, width)

    occ_own = occupied_coeff * occupied_domain[0, 0].astype(BF16)
    occ_by = {s: swap(occ_own, "orb", orb_count, s) if s else occ_own for s in order}
    occ_orb = [occ_by[s] for s in range(orb_count)]

    def raw_piece(s):
        return lax.dynamic_slice_in_dim(raw_all, (orb ^ s) * share, share, 0)

    raw_by = {s: swap(raw_piece(s), "orb", orb_count, s) if s else raw_piece(s) for s in [1, 2, 3, 0]}
    raw = [raw_by[s] for s in range(orb_count)]

    occ_stack = pl.pallas_call(
        stack_kernel,
        out_shape=jax.ShapeDtypeStruct((orb_count, block, block), BF16),
        in_specs=[vmem()] * orb_count,
        out_specs=vmem(),
        compiler_params=pltpu.CompilerParams(vmem_limit_bytes=VMEM_LIMIT),
    )(*occ_orb)
    occ_chip = [occ_stack] + [swap(occ_stack, "ao", ao_count, 2 * t) for t in range(1, chips)]
    occ = []
    for piece in occ_chip:
        occ += [piece, swap(piece, "ao", ao_count, 1)]

    scalars = jnp.concatenate(
        [
            partner[0] ^ ao,
            (jnp.arange(slots, dtype=jnp.int32) < pair_count[0]).astype(jnp.int32),
            orb.astype(jnp.int32)[None],
        ]
    )
    halves = pl.pallas_call(
        functools.partial(half_kernel, orb_count, ao_count),
        out_shape=[jax.ShapeDtypeStruct((share, block, width), BF16)] * orb_count,
        in_specs=[smem()] + [vmem()] * (orb_count + ao_count),
        out_specs=[vmem()] * orb_count,
        scratch_shapes=[
            pltpu.VMEM((ao_count, orb_count, block, block), BF16),
            pltpu.VMEM((orb_count * slots * rows, orb_count * block), BF16),
        ],
        compiler_params=pltpu.CompilerParams(vmem_limit_bytes=VMEM_LIMIT),
        cost_estimate=pl.CostEstimate(
            flops=2 * share * orb_count * orb_count * slots * rows * block * width,
            bytes_accessed=2 * 1024 * 1024,
            transcendentals=0,
        ),
    )(scalars, *raw, *occ)

    virtual_width = virtual_coeff.shape[1]
    per_shard = ao_count // aux_count
    aux_at, ao_at = (x.astype(jnp.int32)[None] for x in (aux, ao))
    masked = pl.pallas_call(
        functools.partial(mask_kernel, per_shard),
        out_shape=jax.ShapeDtypeStruct(virtual_coeff.shape, BF16),
        in_specs=[smem(), smem(), vmem(), pl.BlockSpec(memory_space=pl.ANY)],
        out_specs=vmem(),
        compiler_params=pltpu.CompilerParams(vmem_limit_bytes=VMEM_LIMIT),
    )(aux_at, virtual_domain, virtual_coeff, occ_chip[-1])
    vir = [masked] + [swap(masked, "aux", aux_count, s) for s in range(1, aux_count)]
    virtual = pl.pallas_call(
        functools.partial(virtual_kernel, aux_count, per_shard),
        out_shape=jax.ShapeDtypeStruct((ao_count, block, virtual_width), BF16),
        in_specs=[smem()] * 2 + [vmem()] * aux_count,
        out_specs=vmem(),
        compiler_params=pltpu.CompilerParams(vmem_limit_bytes=VMEM_LIMIT),
        cost_estimate=pl.CostEstimate(
            flops=0,
            bytes_accessed=2 * ao_count * block * virtual_width,
            transcendentals=0,
        ),
    )(aux_at, ao_at, *vir)

    pieces = {}
    result, token = [], None

    def gather(s):
        mine = swap(halves[s], "orb", orb_count, s) if s else halves[s]
        pieces[s] = []
        sent = mine
        if s == orb_count - 1:
            sent = pl.pallas_call(
                gate_kernel,
                out_shape=jax.ShapeDtypeStruct(mine.shape, BF16),
                in_specs=[vmem(), pl.BlockSpec(memory_space=pl.ANY)],
                out_specs=vmem(),
                compiler_params=pltpu.CompilerParams(vmem_limit_bytes=VMEM_LIMIT),
            )(mine, token)
        for part in [mine] + [swap(sent, "ao", ao_count, 2 * t) for t in range(1, chips)]:
            pieces[s] += [part, swap(part, "ao", ao_count, 1)]

    for distances in [[0], [1, 2, 3]]:
        for s in distances:
            gather(s)
        taken = [part for s in distances for part in pieces[s]]
        made, token = pl.pallas_call(
                functools.partial(final_kernel, ao_count, distances),
                out_shape=[
                    jax.ShapeDtypeStruct((slab_rows, block, virtual_width), BF16),
                    jax.ShapeDtypeStruct((8, 128), F32),
                ],
                in_specs=[smem()] + [vmem()] * (1 + len(taken))
                + [pl.BlockSpec(memory_space=pl.ANY)] * len(result),
                out_specs=[pl.BlockSpec(memory_space=pl.ANY), vmem()],
                scratch_shapes=[
                    pltpu.VMEM((len(distances), share, block, virtual_width), BF16),
                    pltpu.SemaphoreType.DMA((len(distances),)),
                ],
                input_output_aliases={2 + len(taken): 0} if result else {},
                compiler_params=pltpu.CompilerParams(vmem_limit_bytes=VMEM_LIMIT),
                cost_estimate=pl.CostEstimate(
                    flops=2 * len(distances) * share * block * ao_count * block * virtual_width,
                    bytes_accessed=len(distances) * 2 * 1024 * 1024,
                    transcendentals=0,
                ),
            )(orb.astype(jnp.int32)[None], virtual, *taken, *result)
        result = [made]
    return result[0]


def solution(mesh):
    placed = (
        P("aux", "ao", None, "orb", None),
        P("ao", None),
        P("ao"),
        P("ao", "orb"),
        P("ao", "orb"),
        P("aux", "ao"),
        P(None, "ao"),
    )
    sizes = tuple(mesh.shape[name] for name in ("aux", "ao", "orb"))
    return jax.shard_map(
        functools.partial(local, sizes),
        mesh=mesh,
        in_specs=placed,
        out_specs=P("aux", "orb", "ao"),
        check_vma=False,
    )
```

```python
import functools

import jax
import jax.numpy as jnp
from jax import lax
from jax.experimental import pallas as pl
from jax.experimental.pallas import tpu as pltpu
from jax.sharding import PartitionSpec as P

BF16 = jnp.bfloat16
F32 = jnp.float32
VMEM_LIMIT = 32 * 1024 * 1024


def swap(x, axis, size, distance):
    return lax.ppermute(x, axis, [(i, i ^ distance) for i in range(size)])


def vmem():
    return pl.BlockSpec(memory_space=pltpu.VMEM)


def smem():
    return pl.BlockSpec(memory_space=pltpu.SMEM)


def stack_kernel(*refs):
    for j, part in enumerate(refs[:-1]):
        refs[-1][j] = part[...]


def half_kernel(orb_count, ao_count, scalars, *refs):
    raw = refs[:orb_count]
    occ = refs[orb_count : orb_count + ao_count]
    outs = refs[orb_count + ao_count : 2 * orb_count + ao_count]
    occ_all, left = refs[2 * orb_count + ao_count :]
    slabs, slots, rows, width = raw[0].shape
    block = occ[0].shape[1]
    for t in range(ao_count):
        occ_all[t] = occ[t][...]
    orb = scalars[2 * slots]
    for s in range(orb_count):
        start = pl.multiple_of((orb ^ s) * rows, rows)
        for k in range(slots):
            live = (scalars[slots + k]).astype(F32).astype(BF16)
            to = (s * slots + k) * rows
            for j in range(orb_count):
                part = occ_all[scalars[k], j, pl.ds(start, rows), :]
                left[to : to + rows, j * block : (j + 1) * block] = part * live
    right = jnp.concatenate(
        [
            jnp.concatenate(
                [raw[s][p].reshape(slots * rows, width) for s in range(orb_count)], axis=0
            )
            for p in range(slabs)
        ],
        axis=1,
    )
    wide = lax.dot_general(
        left[...], right, (((0,), (0,)), ((), ())), preferred_element_type=F32
    ).astype(BF16)
    for j in range(orb_count):
        for p in range(slabs):
            outs[j][p] = wide[j * block : (j + 1) * block, p * width : (p + 1) * width]


def mask_kernel(per_shard, aux, domain, coeff, after, out, held, sem):
    copy = pltpu.make_async_copy(coeff, held, sem)
    copy.start()
    copy.wait()
    width = held.shape[1] // domain.shape[1]
    block = held.shape[0] // per_shard
    for b in range(per_shard):
        for c in range(domain.shape[1]):
            at = (slice(b * block, (b + 1) * block), slice(c * width, (c + 1) * width))
            mask = domain[aux[0] * per_shard + b, c].astype(F32).astype(BF16)
            out[at] = held[at] * mask


def virtual_kernel(aux_count, per_shard, aux, ao, *refs):
    shards, out = refs[:aux_count], refs[aux_count]
    block = out.shape[1]
    for s in range(aux_count):
        for b in range(per_shard):
            out[((aux[0] ^ s) * per_shard + b) ^ ao[0]] = shards[s][b * block : (b + 1) * block]


def final_kernel(ao_count, distances, orb, virtual, *refs):
    halves, (out, token, made, sems) = refs[: ao_count * len(distances)], refs[-4:]
    slabs, rows, block = halves[0].shape
    right = virtual[...].reshape(ao_count * block, virtual.shape[2])
    copies = []
    for w, s in enumerate(distances):
        left = jnp.concatenate(
            [h[...].reshape(slabs * rows, block) for h in halves[w * ao_count : (w + 1) * ao_count]],
            axis=1,
        )
        wide = jnp.dot(left, right, preferred_element_type=F32)
        made[w] = wide.astype(made.dtype).reshape(made.shape[1:])
        start = pl.multiple_of((orb[0] ^ s) * slabs, slabs)
        copy = pltpu.make_async_copy(made.at[w], out.at[pl.ds(start, slabs)], sems.at[w])
        copy.start()
        copies.append(copy)
    for copy in copies:
        copy.wait()
    token[...] = jnp.zeros_like(token)


def gate_kernel(part, after, out):
    out[...] = part[...]


def gate(part, after):
    return pl.pallas_call(
        gate_kernel,
        out_shape=jax.ShapeDtypeStruct(part.shape, BF16),
        in_specs=[vmem(), pl.BlockSpec(memory_space=pl.ANY)],
        out_specs=vmem(),
        compiler_params=pltpu.CompilerParams(vmem_limit_bytes=VMEM_LIMIT),
    )(part, after)


def local(
    sizes, integrals, partner, pair_count, occupied_coeff, occupied_domain, virtual_coeff, virtual_domain
):
    aux_count, ao_count, orb_count = sizes
    chips = ao_count // 2
    aux, ao, orb = (lax.axis_index(name) for name in ("aux", "ao", "orb"))
    slab_rows, _, slots, rows, width = integrals.shape
    block = occupied_coeff.shape[0]
    share = slab_rows // orb_count
    order = [1, 2, 3, 0]
    raw_all = integrals.reshape(slab_rows, slots, rows, width)

    occ_own = occupied_coeff * occupied_domain[0, 0].astype(BF16)
    occ_by = {s: swap(occ_own, "orb", orb_count, s) if s else occ_own for s in order}
    occ_orb = [occ_by[s] for s in range(orb_count)]

    def raw_piece(s):
        return lax.dynamic_slice_in_dim(raw_all, (orb ^ s) * share, share, 0)

    raw_by = {s: swap(raw_piece(s), "orb", orb_count, s) if s else raw_piece(s) for s in [1, 2, 3, 0]}
    raw = [raw_by[s] for s in range(orb_count)]

    occ_stack = pl.pallas_call(
        stack_kernel,
        out_shape=jax.ShapeDtypeStruct((orb_count, block, block), BF16),
        in_specs=[vmem()] * orb_count,
        out_specs=vmem(),
        compiler_params=pltpu.CompilerParams(vmem_limit_bytes=VMEM_LIMIT),
    )(*occ_orb)
    occ_chip = [occ_stack] + [swap(occ_stack, "ao", ao_count, 2 * t) for t in range(1, chips)]
    occ = []
    for piece in occ_chip:
        occ += [piece, swap(piece, "ao", ao_count, 1)]

    scalars = jnp.concatenate(
        [
            partner[0] ^ ao,
            (jnp.arange(slots, dtype=jnp.int32) < pair_count[0]).astype(jnp.int32),
            orb.astype(jnp.int32)[None],
        ]
    )
    halves = pl.pallas_call(
        functools.partial(half_kernel, orb_count, ao_count),
        out_shape=[jax.ShapeDtypeStruct((share, block, width), BF16)] * orb_count,
        in_specs=[smem()] + [vmem()] * (orb_count + ao_count),
        out_specs=[vmem()] * orb_count,
        scratch_shapes=[
            pltpu.VMEM((ao_count, orb_count, block, block), BF16),
            pltpu.VMEM((orb_count * slots * rows, orb_count * block), BF16),
        ],
        compiler_params=pltpu.CompilerParams(vmem_limit_bytes=VMEM_LIMIT),
        cost_estimate=pl.CostEstimate(
            flops=2 * share * orb_count * orb_count * slots * rows * block * width,
            bytes_accessed=2 * 1024 * 1024,
            transcendentals=0,
        ),
    )(scalars, *raw, *occ)

    moved = {s: swap(halves[s], "orb", orb_count, s) if s else halves[s] for s in range(orb_count)}

    virtual_width = virtual_coeff.shape[1]
    per_shard = ao_count // aux_count
    aux_at, ao_at = (x.astype(jnp.int32)[None] for x in (aux, ao))
    masked = pl.pallas_call(
        functools.partial(mask_kernel, per_shard),
        out_shape=jax.ShapeDtypeStruct(virtual_coeff.shape, BF16),
        in_specs=[
            smem(),
            smem(),
            pl.BlockSpec(memory_space=pltpu.HBM),
            pl.BlockSpec(memory_space=pl.ANY),
        ],
        out_specs=vmem(),
        scratch_shapes=[pltpu.VMEM(virtual_coeff.shape, BF16), pltpu.SemaphoreType.DMA],
        compiler_params=pltpu.CompilerParams(vmem_limit_bytes=VMEM_LIMIT),
    )(aux_at, virtual_domain, virtual_coeff, occ_chip[-1])
    vir = [masked] + [swap(masked, "aux", aux_count, s) for s in range(1, aux_count)]
    virtual = pl.pallas_call(
        functools.partial(virtual_kernel, aux_count, per_shard),
        out_shape=jax.ShapeDtypeStruct((ao_count, block, virtual_width), BF16),
        in_specs=[smem()] * 2 + [vmem()] * aux_count,
        out_specs=vmem(),
        compiler_params=pltpu.CompilerParams(vmem_limit_bytes=VMEM_LIMIT),
        cost_estimate=pl.CostEstimate(
            flops=0,
            bytes_accessed=2*1024*1024,
            transcendentals=0,
        ),
    )(aux_at, ao_at, *vir)

    pieces = {}
    result, tokens = [], []

    def gather(s):
        mine = moved[s]
        last = s == orb_count - 1
        pieces[s] = []
        over = [mine] + [
            swap(mine, "ao", ao_count, 2 * t) for t in range(1, chips)
        ]
        for t, part in enumerate(over):
            sent = part
            if last and t > 0:
                sent = gate(part, tokens[0])
            pieces[s] += [part, swap(sent, "ao", ao_count, 1)]

    for distances in [[0, 1, 2], [3]]:
        for s in distances:
            gather(s)
        taken = [part for s in distances for part in pieces[s]]
        made, token = pl.pallas_call(
                functools.partial(final_kernel, ao_count, distances),
                out_shape=[
                    jax.ShapeDtypeStruct((slab_rows, block, virtual_width), BF16),
                    jax.ShapeDtypeStruct((8, 128), F32),
                ],
                in_specs=[smem()] + [vmem()] * (1 + len(taken))
                + [pl.BlockSpec(memory_space=pl.ANY)] * len(result),
                out_specs=[pl.BlockSpec(memory_space=pl.ANY), vmem()],
                scratch_shapes=[
                    pltpu.VMEM((len(distances), share, block, virtual_width), BF16),
                    pltpu.SemaphoreType.DMA((len(distances),)),
                ],
                input_output_aliases={2 + len(taken): 0} if result else {},
                compiler_params=pltpu.CompilerParams(vmem_limit_bytes=VMEM_LIMIT),
                cost_estimate=pl.CostEstimate(
                    flops=2*1024*1024,
                    bytes_accessed=2*1024*1024,
                    transcendentals=0,
                ),
            )(orb.astype(jnp.int32)[None], virtual, *taken, *result)
        result = [made]
        tokens.append(token)
    return result[0]


def solution(mesh):
    placed = (
        P("aux", "ao", None, "orb", None),
        P("ao", None),
        P("ao"),
        P("ao", "orb"),
        P("ao", "orb"),
        P("aux", "ao"),
        P(None, "ao"),
    )
    sizes = tuple(mesh.shape[name] for name in ("aux", "ao", "orb"))
    return jax.shard_map(
        functools.partial(local, sizes),
        mesh=mesh,
        in_specs=placed,
        out_specs=P("aux", "orb", "ao"),
        check_vma=False,
    )
```

```python
import functools

import jax
import jax.numpy as jnp
from jax import lax
from jax.experimental import pallas as pl
from jax.experimental.pallas import tpu as pltpu
from jax.sharding import PartitionSpec as P

BF16 = jnp.bfloat16
F32 = jnp.float32
VMEM_LIMIT = 32 * 1024 * 1024
CHUNKS = 2
STEPS = 2


def swap(x, axis, size, distance):
    return lax.ppermute(x, axis, [(i, i ^ distance) for i in range(size)])


def behind(part, *after):
    return lax.optimization_barrier((part, *after))[0]


def vmem():
    return pl.BlockSpec(memory_space=pltpu.VMEM)


def smem():
    return pl.BlockSpec(memory_space=pltpu.SMEM)


def anywhere():
    return pl.BlockSpec(memory_space=pl.ANY)


def as_bf16(value):
    return value.astype(F32).astype(BF16)


def call(body, flops, touched, **rest):
    return pl.pallas_call(
        body,
        compiler_params=pltpu.CompilerParams(vmem_limit_bytes=VMEM_LIMIT),
        cost_estimate=pl.CostEstimate(
            flops=flops, bytes_accessed=touched, transcendentals=0
        ),
        **rest,
    )


def pair_kernel(first, second, out):
    out[0] = first[...]
    out[1] = second[...]


def left_kernel(ao_count, slots, rows, orb, ao, partner, pair_count, *refs):
    occ, out, occ_all, upright = refs[:ao_count], refs[-3], refs[-2], refs[-1]
    blocks, block, _ = occ[0].shape
    for t in range(ao_count):
        occ_all[t] = occ[t][...]
    for k in range(slots):
        live = as_bf16((k < pair_count[0]).astype(jnp.int32))
        source = partner[0, k] ^ ao[0]
        for s in range(block // rows):
            start = pl.multiple_of((orb[0] ^ s) * rows, rows)
            to = (s * slots + k) * rows
            for w in range(blocks):
                upright[to : to + rows, w * block : (w + 1) * block] = (
                    occ_all[source, w, pl.ds(start, rows), :] * live
                )
    out[...] = upright[...].T


def half_kernel(left, *refs):
    raw, outs = refs[:4], refs[4:]
    slabs, block, width = outs[0].shape
    slot_rows = raw[0].shape[0] // slabs
    right = jnp.concatenate(
        [
            jnp.concatenate(
                [part[p * slot_rows : (p + 1) * slot_rows, :] for part in raw], axis=0
            )
            for p in range(slabs)
        ],
        axis=1,
    )
    wide = jnp.dot(left[...], right, preferred_element_type=F32).astype(BF16)
    for w in range(len(outs)):
        for p in range(slabs):
            outs[w][p] = wide[w * block : (w + 1) * block, p * width : (p + 1) * width]


def virtual_kernel(aux_count, per_shard, aux, ao, domain, *refs):
    shards, out = refs[:aux_count], refs[aux_count]
    block = out.shape[1]
    width = out.shape[2] // domain.shape[1]
    for s in range(aux_count):
        for b in range(per_shard):
            n = (aux[0] ^ s) * per_shard + b
            for c in range(domain.shape[1]):
                cols = slice(c * width, (c + 1) * width)
                out[n ^ ao[0], :, cols] = shards[s][
                    b * block : (b + 1) * block, cols
                ] * as_bf16(domain[n, c])


def final_kernel(ao_count, count, places, virtual, *refs):
    halves, out, made, sems = refs[: ao_count * count], refs[-3], refs[-2], refs[-1]
    slabs, rows, block = halves[0].shape
    step = slabs // STEPS
    right = virtual[...].reshape(ao_count * block, virtual.shape[2])
    copies = []
    for w in range(count):
        for g in range(STEPS):
            part = pl.ds(g * step, step)
            left = jnp.concatenate(
                [
                    h[part].reshape(step * rows, block)
                    for h in halves[w * ao_count : (w + 1) * ao_count]
                ],
                axis=1,
            )
            wide = jnp.dot(left, right, preferred_element_type=F32)
            made[w, part] = wide.astype(made.dtype).reshape(step, rows, virtual.shape[2])
            copy = pltpu.make_async_copy(
                made.at[w, part],
                out.at[pl.ds(places[w] * slabs + g * step, step)],
                sems.at[w * STEPS + g],
            )
            copy.start()
            copies.append(copy)
    for copy in copies:
        copy.wait()


def local(
    sizes, integrals, partner, pair_count, occupied_coeff, occupied_domain, virtual_coeff, virtual_domain
):
    aux_count, ao_count, orb_count = sizes
    chips = ao_count // 2
    aux, ao, orb = (
        lax.axis_index(name).astype(jnp.int32)[None] for name in ("aux", "ao", "orb")
    )
    slab_rows, _, slots, rows, width = integrals.shape
    block = occupied_coeff.shape[0]
    share = slab_rows // (2 * CHUNKS)
    piece_rows = share * slots * rows
    odd = orb[0] % 2

    def array(*shape):
        return jax.ShapeDtypeStruct(shape, BF16)

    flat = integrals.reshape(slab_rows * slots * rows, width)

    def cut(parity, c):
        return lax.dynamic_slice_in_dim(flat, (parity * CHUNKS + c) * piece_rows, piece_rows, 0)

    kept = [cut(odd, c) for c in range(CHUNKS)]
    given = [cut(1 - odd, c) for c in range(CHUNKS)]
    beside = [swap(part, "orb", orb_count, 1) for part in given]
    across, crossed = [], []
    for c in range(CHUNKS):
        one, two = kept[c], beside[c]
        if c:
            two = behind(two, crossed[-1], across[-1])
        crossed.append(swap(one, "orb", orb_count, 2))
        across.append(swap(two, "orb", orb_count, 2))

    occ_own = occupied_coeff * occupied_domain[0, 0].astype(BF16)
    occ_pair = call(
        pair_kernel,
        0,
        8 * block * block,
        out_shape=array(2, block, block),
        in_specs=[vmem()] * 2,
        out_specs=vmem(),
    )(occ_own, swap(occ_own, "orb", orb_count, 1))
    occ = []
    for part in [occ_pair] + [swap(occ_pair, "ao", ao_count, 2 * t) for t in range(1, chips)]:
        occ += [part, swap(part, "ao", ao_count, 1)]
    left = call(
        functools.partial(left_kernel, ao_count, slots, rows),
        2 * block * slots * block,
        8 * block * slots * block,
        out_shape=array(2 * block, slots * block),
        in_specs=[smem()] * 4 + [vmem()] * ao_count,
        out_specs=vmem(),
        scratch_shapes=[
            pltpu.VMEM((ao_count, 2, block, block), BF16),
            pltpu.VMEM((slots * block, 2 * block), BF16),
        ],
    )(orb, ao, partner, pair_count, *occ)

    held = behind(virtual_coeff, crossed[0])
    vir = [virtual_coeff] + [swap(held, "aux", aux_count, s) for s in range(1, aux_count)]
    virtual_width = virtual_coeff.shape[1]
    virtual = call(
        functools.partial(virtual_kernel, aux_count, ao_count // aux_count),
        1024*1024,
        1024*1024,
        out_shape=array(ao_count, block, virtual_width),
        in_specs=[smem()] * 3 + [vmem()] * aux_count,
        out_specs=vmem(),
    )(aux, ao, virtual_domain, *vir)

    own, back = [], []
    for c in range(CHUNKS):
        mine, sent = call(
            half_kernel,
            2 * share * 2 * block * slots * block * width,
            12 * piece_rows * width,
            out_shape=[array(share, block, width)] * 2,
            in_specs=[vmem()] * 5,
            out_specs=[vmem()] * 2,
        )(left, kept[c], beside[c], crossed[c], across[c])
        own.append((odd * CHUNKS + c, mine))
        back.append(((1 - odd) * CHUNKS + c, swap(sent, "orb", orb_count, 1)))

    def gathered(mine):
        pieces = []
        for part in [mine] + [swap(mine, "ao", ao_count, 2 * t) for t in range(1, chips)]:
            pieces += [part, swap(part, "ao", ao_count, 1)]
        return pieces

    result = []
    for group in ([own[0], back[0]], own[1:], back[1:]):
        taken = [part for _, mine in group for part in gathered(mine)]
        result = [
            call(
                functools.partial(final_kernel, ao_count, len(group)),
                2*1024*1024 * len(group),
                2*1024*1024 * len(group),
                out_shape=array(slab_rows, block, virtual_width),
                in_specs=[smem()] + [vmem()] * (1 + len(taken)) + [anywhere()] * len(result),
                out_specs=anywhere(),
                scratch_shapes=[
                    pltpu.VMEM((len(group), share, block, virtual_width), BF16),
                    pltpu.SemaphoreType.DMA((len(group) * STEPS,)),
                ],
                input_output_aliases={2 + len(taken): 0} if result else {},
            )(jnp.stack([place for place, _ in group]), virtual, *taken, *result)
        ]
    return result[0]


def solution(mesh):
    placed = (
        P("aux", "ao", None, "orb", None),
        P("ao", None),
        P("ao"),
        P("ao", "orb"),
        P("ao", "orb"),
        P("aux", "ao"),
        P(None, "ao"),
    )
    sizes = tuple(mesh.shape[name] for name in ("aux", "ao", "orb"))
    return jax.shard_map(
        functools.partial(local, sizes),
        mesh=mesh,
        in_specs=placed,
        out_specs=P("aux", "orb", "ao"),
        check_vma=False,
    )
```

```python
import functools

import jax
import jax.numpy as jnp
from jax import lax
from jax.experimental import pallas as pl
from jax.experimental.pallas import tpu as pltpu
from jax.sharding import PartitionSpec as P

BF16 = jnp.bfloat16
F32 = jnp.float32
VMEM_LIMIT = 32 * 1024 * 1024
GROUPS = [[0, 1], [2, 3]]


def swap(x, axis, size, distance):
    return lax.ppermute(x, axis, [(i, i ^ distance) for i in range(size)])


def vmem():
    return pl.BlockSpec(memory_space=pltpu.VMEM)


def smem():
    return pl.BlockSpec(memory_space=pltpu.SMEM)


def stack_kernel(*refs):
    for j, part in enumerate(refs[:-1]):
        refs[-1][j] = part[...]


def behind(part, after):
    return lax.optimization_barrier((part, after))[0]


def half_kernel(orb_count, ao_count, scalars, *refs):
    raw = refs[:orb_count]
    occ = refs[orb_count : orb_count + ao_count]
    outs = refs[orb_count + ao_count : 2 * orb_count + ao_count]
    occ_all, left = refs[2 * orb_count + ao_count :]
    slabs, slots, rows, width = raw[0].shape
    block = occ[0].shape[1]
    for t in range(ao_count):
        occ_all[t] = occ[t][...]
    orb = scalars[2 * slots]
    for s in range(orb_count):
        start = pl.multiple_of((orb ^ s) * rows, rows)
        for k in range(slots):
            live = (scalars[slots + k]).astype(F32).astype(BF16)
            to = (s * slots + k) * rows
            for j in range(orb_count):
                part = occ_all[scalars[k], j, pl.ds(start, rows), :]
                left[to : to + rows, j * block : (j + 1) * block] = part * live
    right = jnp.concatenate(
        [
            jnp.concatenate(
                [raw[s][p].reshape(slots * rows, width) for s in range(orb_count)], axis=0
            )
            for p in range(slabs)
        ],
        axis=1,
    )
    wide = lax.dot_general(
        left[...], right, (((0,), (0,)), ((), ())), preferred_element_type=F32
    ).astype(BF16)
    for j in range(orb_count):
        for p in range(slabs):
            outs[j][p] = wide[j * block : (j + 1) * block, p * width : (p + 1) * width]


def mask_kernel(per_shard, aux, domain, coeff, after, out, held, sem):
    copy = pltpu.make_async_copy(coeff, held, sem)
    copy.start()
    copy.wait()
    width = held.shape[1] // domain.shape[1]
    block = held.shape[0] // per_shard
    for b in range(per_shard):
        for c in range(domain.shape[1]):
            at = (slice(b * block, (b + 1) * block), slice(c * width, (c + 1) * width))
            mask = domain[aux[0] * per_shard + b, c].astype(F32).astype(BF16)
            out[at] = held[at] * mask


def virtual_kernel(aux_count, per_shard, aux, ao, *refs):
    shards, out = refs[:aux_count], refs[aux_count]
    block = out.shape[1]
    for s in range(aux_count):
        for b in range(per_shard):
            out[((aux[0] ^ s) * per_shard + b) ^ ao[0]] = shards[s][b * block : (b + 1) * block]


def final_kernel(ao_count, distances, orb, virtual, *refs):
    halves, (made, sems) = refs[: ao_count * len(distances)], refs[-2:]
    out = refs[-3] if refs[-3].ndim == 3 else refs[-4]
    slabs, rows, block = halves[0].shape
    right = virtual[...].reshape(ao_count * block, virtual.shape[2])
    copies = []
    for w, s in enumerate(distances):
        left = jnp.concatenate(
            [h[...].reshape(slabs * rows, block) for h in halves[w * ao_count : (w + 1) * ao_count]],
            axis=1,
        )
        wide = jnp.dot(left, right, preferred_element_type=F32)
        made[w] = wide.astype(made.dtype).reshape(made.shape[1:])
        start = pl.multiple_of((orb[0] ^ s) * slabs, slabs)
        copy = pltpu.make_async_copy(made.at[w], out.at[pl.ds(start, slabs)], sems.at[w])
        copy.start()
        copies.append(copy)
    for copy in copies:
        copy.wait()
    if refs[-3].ndim == 2:
        refs[-3][...] = jnp.zeros_like(refs[-3])


def gate_kernel(part, after, out):
    out[...] = part[...]


def gate(part, after):
    return pl.pallas_call(
        gate_kernel,
        out_shape=jax.ShapeDtypeStruct(part.shape, BF16),
        in_specs=[vmem(), pl.BlockSpec(memory_space=pl.ANY)],
        out_specs=vmem(),
        compiler_params=pltpu.CompilerParams(vmem_limit_bytes=VMEM_LIMIT),
    )(part, after)


def local(
    sizes, integrals, partner, pair_count, occupied_coeff, occupied_domain, virtual_coeff, virtual_domain
):
    aux_count, ao_count, orb_count = sizes
    chips = ao_count // 2
    aux, ao, orb = (lax.axis_index(name) for name in ("aux", "ao", "orb"))
    slab_rows, _, slots, rows, width = integrals.shape
    block = occupied_coeff.shape[0]
    share = slab_rows // orb_count
    order = [1, 2, 3, 0]
    raw_all = integrals.reshape(slab_rows, slots, rows, width)

    occ_own = occupied_coeff * occupied_domain[0, 0].astype(BF16)
    occ_by = {s: swap(occ_own, "orb", orb_count, s) if s else occ_own for s in order}
    occ_orb = [occ_by[s] for s in range(orb_count)]

    def raw_piece(s):
        return lax.dynamic_slice_in_dim(raw_all, (orb ^ s) * share, share, 0)

    raw_by = {s: swap(behind(raw_piece(s), occ_by[1]) if s == 1 else raw_piece(s), "orb", orb_count, s)
        if s
        else raw_piece(s) for s in [1, 2, 3, 0]}
    raw = [raw_by[s] for s in range(orb_count)]

    occ_stack = pl.pallas_call(
        stack_kernel,
        out_shape=jax.ShapeDtypeStruct((orb_count, block, block), BF16),
        in_specs=[vmem()] * orb_count,
        out_specs=vmem(),
        compiler_params=pltpu.CompilerParams(vmem_limit_bytes=VMEM_LIMIT),
    )(*occ_orb)
    occ_chip = [occ_stack] + [swap(occ_stack, "ao", ao_count, 2 * t) for t in range(1, chips)]
    occ = []
    for piece in occ_chip:
        occ += [piece, swap(piece, "ao", ao_count, 1)]

    scalars = jnp.concatenate(
        [
            partner[0] ^ ao,
            (jnp.arange(slots, dtype=jnp.int32) < pair_count[0]).astype(jnp.int32),
            orb.astype(jnp.int32)[None],
        ]
    )
    halves = pl.pallas_call(
        functools.partial(half_kernel, orb_count, ao_count),
        out_shape=[jax.ShapeDtypeStruct((share, block, width), BF16)] * orb_count,
        in_specs=[smem()] + [vmem()] * (orb_count + ao_count),
        out_specs=[vmem()] * orb_count,
        scratch_shapes=[
            pltpu.VMEM((ao_count, orb_count, block, block), BF16),
            pltpu.VMEM((orb_count * slots * rows, orb_count * block), BF16),
        ],
        compiler_params=pltpu.CompilerParams(vmem_limit_bytes=VMEM_LIMIT),
        cost_estimate=pl.CostEstimate(
            flops=2 * share * orb_count * orb_count * slots * rows * block * width,
            bytes_accessed=2 * 1024 * 1024,
            transcendentals=0,
        ),
    )(scalars, *raw, *occ)

    moved = {s: swap(halves[s], "orb", orb_count, s) if s else halves[s] for s in range(orb_count)}

    virtual_width = virtual_coeff.shape[1]
    per_shard = ao_count // aux_count
    aux_at, ao_at = (x.astype(jnp.int32)[None] for x in (aux, ao))
    masked = pl.pallas_call(
        functools.partial(mask_kernel, per_shard),
        out_shape=jax.ShapeDtypeStruct(virtual_coeff.shape, BF16),
        in_specs=[
            smem(),
            smem(),
            pl.BlockSpec(memory_space=pltpu.HBM),
            pl.BlockSpec(memory_space=pl.ANY),
        ],
        out_specs=vmem(),
        scratch_shapes=[pltpu.VMEM(virtual_coeff.shape, BF16), pltpu.SemaphoreType.DMA],
        compiler_params=pltpu.CompilerParams(vmem_limit_bytes=VMEM_LIMIT),
    )(aux_at, virtual_domain, virtual_coeff, occ_chip[-1])
    vir = [masked] + [swap(masked, "aux", aux_count, s) for s in range(1, aux_count)]
    virtual = pl.pallas_call(
        functools.partial(virtual_kernel, aux_count, per_shard),
        out_shape=jax.ShapeDtypeStruct((ao_count, block, virtual_width), BF16),
        in_specs=[smem()] * 2 + [vmem()] * aux_count,
        out_specs=vmem(),
        compiler_params=pltpu.CompilerParams(vmem_limit_bytes=VMEM_LIMIT),
        cost_estimate=pl.CostEstimate(
            flops=0,
            bytes_accessed=2*1024*1024,
            transcendentals=0,
        ),
    )(aux_at, ao_at, *vir)

    pieces = {}
    result, tokens = [], []

    def gather(s):
        mine = moved[s]
        last = s == orb_count - 1
        pieces[s] = []
        over = [mine] + [
            swap(mine, "ao", ao_count, 2 * t) for t in range(1, chips)
        ]
        for t, part in enumerate(over):
            sent = part
            if last and t > 0:
                sent = gate(part, tokens[0])
            pieces[s] += [part, swap(sent, "ao", ao_count, 1)]

    for distances in GROUPS:
        for s in distances:
            gather(s)
        taken = [part for s in distances for part in pieces[s]]
        made, *token = pl.pallas_call(
                functools.partial(final_kernel, ao_count, distances),
                out_shape=[
                    jax.ShapeDtypeStruct((slab_rows, block, virtual_width), BF16),
                ]
                + [jax.ShapeDtypeStruct((8, 128), F32)] * (distances != GROUPS[-1]),
                in_specs=[smem()] + [vmem()] * (1 + len(taken))
                + [pl.BlockSpec(memory_space=pl.ANY)] * len(result),
                out_specs=[pl.BlockSpec(memory_space=pl.ANY)]
                + [vmem()] * (distances != GROUPS[-1]),
                scratch_shapes=[
                    pltpu.VMEM((len(distances), share, block, virtual_width), BF16),
                    pltpu.SemaphoreType.DMA((len(distances),)),
                ],
                input_output_aliases={2 + len(taken): 0} if result else {},
                compiler_params=pltpu.CompilerParams(vmem_limit_bytes=VMEM_LIMIT),
                cost_estimate=pl.CostEstimate(
                    flops=2*1024*1024,
                    bytes_accessed=2*1024*1024,
                    transcendentals=0,
                ),
            )(orb.astype(jnp.int32)[None], virtual, *taken, *result)
        result = [made]
        tokens += token
    return result[0]


def solution(mesh):
    placed = (
        P("aux", "ao", None, "orb", None),
        P("ao", None),
        P("ao"),
        P("ao", "orb"),
        P("ao", "orb"),
        P("aux", "ao"),
        P(None, "ao"),
    )
    sizes = tuple(mesh.shape[name] for name in ("aux", "ao", "orb"))
    return jax.shard_map(
        functools.partial(local, sizes),
        mesh=mesh,
        in_specs=placed,
        out_specs=P("aux", "orb", "ao"),
        check_vma=False,
    )
```

```python
import functools

import jax
import jax.numpy as jnp
from jax import lax
from jax.experimental import pallas as pl
from jax.experimental.pallas import tpu as pltpu
from jax.sharding import PartitionSpec as P

BF16 = jnp.bfloat16
F32 = jnp.float32
VMEM_LIMIT = 32 * 1024 * 1024
GROUPS = [[0, 1], [2, 3]]


def swap(x, axis, size, distance):
    return lax.ppermute(x, axis, [(i, i ^ distance) for i in range(size)])


def vmem():
    return pl.BlockSpec(memory_space=pltpu.VMEM)


def smem():
    return pl.BlockSpec(memory_space=pltpu.SMEM)


def stack_kernel(*refs):
    for j, part in enumerate(refs[:-1]):
        refs[-1][j] = part[...]


def behind(part, after):
    return lax.optimization_barrier((part, after))[0]


def half_kernel(orb_count, ao_count, scalars, *refs):
    raw = refs[:orb_count]
    occ = refs[orb_count : orb_count + ao_count]
    outs = refs[orb_count + ao_count : 2 * orb_count + ao_count]
    occ_all, left = refs[2 * orb_count + ao_count :]
    slabs, slots, rows, width = raw[0].shape
    block = occ[0].shape[1]
    for t in range(ao_count):
        occ_all[t] = occ[t][...]
    orb = scalars[2 * slots]
    for s in range(orb_count):
        start = pl.multiple_of((orb ^ s) * rows, rows)
        for k in range(slots):
            live = (scalars[slots + k]).astype(F32).astype(BF16)
            to = (s * slots + k) * rows
            for j in range(orb_count):
                part = occ_all[scalars[k], j, pl.ds(start, rows), :]
                left[to : to + rows, j * block : (j + 1) * block] = part * live
    right = jnp.concatenate(
        [
            jnp.concatenate(
                [raw[s][p].reshape(slots * rows, width) for s in range(orb_count)], axis=0
            )
            for p in range(slabs)
        ],
        axis=1,
    )
    wide = lax.dot_general(
        left[...], right, (((0,), (0,)), ((), ())), preferred_element_type=F32
    ).astype(BF16)
    for j in range(orb_count):
        for p in range(slabs):
            outs[j][p] = wide[j * block : (j + 1) * block, p * width : (p + 1) * width]


def mask_kernel(per_shard, aux, domain, coeff, after, out, held, sem):
    copy = pltpu.make_async_copy(coeff, held, sem)
    copy.start()
    copy.wait()
    width = held.shape[1] // domain.shape[1]
    block = held.shape[0] // per_shard
    for b in range(per_shard):
        for c in range(domain.shape[1]):
            at = (slice(b * block, (b + 1) * block), slice(c * width, (c + 1) * width))
            mask = domain[aux[0] * per_shard + b, c].astype(F32).astype(BF16)
            out[at] = held[at] * mask


def virtual_kernel(aux_count, per_shard, aux, ao, *refs):
    shards, out = refs[:aux_count], refs[aux_count]
    block = out.shape[1]
    for s in range(aux_count):
        for b in range(per_shard):
            out[((aux[0] ^ s) * per_shard + b) ^ ao[0]] = shards[s][b * block : (b + 1) * block]


def final_kernel(ao_count, distances, orb, virtual, *refs):
    halves, (made, sems) = refs[: ao_count * len(distances)], refs[-2:]
    out = refs[-3] if refs[-3].ndim == 3 else refs[-4]
    slabs, rows, block = halves[0].shape
    right = virtual[...].reshape(ao_count * block, virtual.shape[2])
    copies = []
    for w, s in enumerate(distances):
        left = jnp.concatenate(
            [h[...].reshape(slabs * rows, block) for h in halves[w * ao_count : (w + 1) * ao_count]],
            axis=1,
        )
        wide = jnp.dot(left, right, preferred_element_type=F32)
        made[w] = wide.astype(made.dtype).reshape(made.shape[1:])
        start = pl.multiple_of((orb[0] ^ s) * slabs, slabs)
        copy = pltpu.make_async_copy(made.at[w], out.at[pl.ds(start, slabs)], sems.at[w])
        copy.start()
        copies.append(copy)
    for copy in copies:
        copy.wait()
    if refs[-3].ndim == 2:
        refs[-3][...] = jnp.zeros_like(refs[-3])


def gate_kernel(part, after, out):
    out[...] = part[...]


def gate(part, after):
    return pl.pallas_call(
        gate_kernel,
        out_shape=jax.ShapeDtypeStruct(part.shape, BF16),
        in_specs=[vmem(), pl.BlockSpec(memory_space=pl.ANY)],
        out_specs=vmem(),
        compiler_params=pltpu.CompilerParams(vmem_limit_bytes=VMEM_LIMIT),
    )(part, after)


def local(
    sizes, integrals, partner, pair_count, occupied_coeff, occupied_domain, virtual_coeff, virtual_domain
):
    aux_count, ao_count, orb_count = sizes
    chips = ao_count // 2
    aux, ao, orb = (lax.axis_index(name) for name in ("aux", "ao", "orb"))
    slab_rows, _, slots, rows, width = integrals.shape
    block = occupied_coeff.shape[0]
    share = slab_rows // orb_count
    order = [1, 2, 3, 0]
    raw_all = integrals.reshape(slab_rows, slots, rows, width)

    occ_own = occupied_coeff * occupied_domain[0, 0].astype(BF16)
    occ_by = {s: swap(occ_own, "orb", orb_count, s) if s else occ_own for s in order}
    occ_orb = [occ_by[s] for s in range(orb_count)]

    def raw_piece(s):
        return lax.dynamic_slice_in_dim(raw_all, (orb ^ s) * share, share, 0)

    raw_by = {s: swap(raw_piece(s), "orb", orb_count, s) if s else raw_piece(s) for s in [1, 2, 3, 0]}
    raw = [raw_by[s] for s in range(orb_count)]

    occ_stack = pl.pallas_call(
        stack_kernel,
        out_shape=jax.ShapeDtypeStruct((orb_count, block, block), BF16),
        in_specs=[vmem()] * orb_count,
        out_specs=vmem(),
        compiler_params=pltpu.CompilerParams(vmem_limit_bytes=VMEM_LIMIT),
    )(*occ_orb)
    occ_chip = [occ_stack] + [swap(occ_stack, "ao", ao_count, 2 * t) for t in range(1, chips)]
    occ = []
    for piece in occ_chip:
        occ += [piece, swap(piece, "ao", ao_count, 1)]

    scalars = jnp.concatenate(
        [
            partner[0] ^ ao,
            (jnp.arange(slots, dtype=jnp.int32) < pair_count[0]).astype(jnp.int32),
            orb.astype(jnp.int32)[None],
        ]
    )
    halves = pl.pallas_call(
        functools.partial(half_kernel, orb_count, ao_count),
        out_shape=[jax.ShapeDtypeStruct((share, block, width), BF16)] * orb_count,
        in_specs=[smem()] + [vmem()] * (orb_count + ao_count),
        out_specs=[vmem()] * orb_count,
        scratch_shapes=[
            pltpu.VMEM((ao_count, orb_count, block, block), BF16),
            pltpu.VMEM((orb_count * slots * rows, orb_count * block), BF16),
        ],
        compiler_params=pltpu.CompilerParams(vmem_limit_bytes=VMEM_LIMIT),
        cost_estimate=pl.CostEstimate(
            flops=2 * share * orb_count * orb_count * slots * rows * block * width,
            bytes_accessed=2 * 1024 * 1024,
            transcendentals=0,
        ),
    )(scalars, *raw, *occ)

    moved = {s: swap(halves[s], "orb", orb_count, s) if s else halves[s] for s in range(orb_count)}

    virtual_width = virtual_coeff.shape[1]
    per_shard = ao_count // aux_count
    aux_at, ao_at = (x.astype(jnp.int32)[None] for x in (aux, ao))
    masked = pl.pallas_call(
        functools.partial(mask_kernel, per_shard),
        out_shape=jax.ShapeDtypeStruct(virtual_coeff.shape, BF16),
        in_specs=[
            smem(),
            smem(),
            pl.BlockSpec(memory_space=pltpu.HBM),
            pl.BlockSpec(memory_space=pl.ANY),
        ],
        out_specs=vmem(),
        scratch_shapes=[pltpu.VMEM(virtual_coeff.shape, BF16), pltpu.SemaphoreType.DMA],
        compiler_params=pltpu.CompilerParams(vmem_limit_bytes=VMEM_LIMIT),
    )(aux_at, virtual_domain, virtual_coeff, occ_chip[-1])
    vir = [masked] + [swap(masked, "aux", aux_count, s) for s in range(1, aux_count)]
    virtual = pl.pallas_call(
        functools.partial(virtual_kernel, aux_count, per_shard),
        out_shape=jax.ShapeDtypeStruct((ao_count, block, virtual_width), BF16),
        in_specs=[smem()] * 2 + [vmem()] * aux_count,
        out_specs=vmem(),
        compiler_params=pltpu.CompilerParams(vmem_limit_bytes=VMEM_LIMIT),
        cost_estimate=pl.CostEstimate(
            flops=0,
            bytes_accessed=2*1024*1024,
            transcendentals=0,
        ),
    )(aux_at, ao_at, *vir)

    pieces = {}
    result, tokens = [], []

    def gather(s):
        mine = moved[s]
        last = s == orb_count - 1
        pieces[s] = []
        over = [mine] + [
            swap(mine, "ao", ao_count, 2 * t) for t in range(1, chips)
        ]
        for t, part in enumerate(over):
            sent = part
            if last and t > 0:
                sent = gate(part, tokens[0])
            pieces[s] += [part, swap(sent, "ao", ao_count, 1)]

    for distances in GROUPS:
        for s in distances:
            gather(s)
        taken = [part for s in distances for part in pieces[s]]
        made, *token = pl.pallas_call(
                functools.partial(final_kernel, ao_count, distances),
                out_shape=[
                    jax.ShapeDtypeStruct((slab_rows, block, virtual_width), BF16),
                ]
                + [jax.ShapeDtypeStruct((8, 128), F32)] * (distances != GROUPS[-1]),
                in_specs=[smem()] + [vmem()] * (1 + len(taken))
                + [pl.BlockSpec(memory_space=pl.ANY)] * len(result),
                out_specs=[pl.BlockSpec(memory_space=pl.ANY)]
                + [vmem()] * (distances != GROUPS[-1]),
                scratch_shapes=[
                    pltpu.VMEM((len(distances), share, block, virtual_width), BF16),
                    pltpu.SemaphoreType.DMA((len(distances),)),
                ],
                input_output_aliases={2 + len(taken): 0} if result else {},
                compiler_params=pltpu.CompilerParams(vmem_limit_bytes=VMEM_LIMIT),
                cost_estimate=pl.CostEstimate(
                    flops=2*1024*1024,
                    bytes_accessed=2*1024*1024,
                    transcendentals=0,
                ),
            )(orb.astype(jnp.int32)[None], virtual, *taken, *result)
        result = [made]
        tokens += token
    return result[0]


def solution(mesh):
    placed = (
        P("aux", "ao", None, "orb", None),
        P("ao", None),
        P("ao"),
        P("ao", "orb"),
        P("ao", "orb"),
        P("aux", "ao"),
        P(None, "ao"),
    )
    sizes = tuple(mesh.shape[name] for name in ("aux", "ao", "orb"))
    return jax.shard_map(
        functools.partial(local, sizes),
        mesh=mesh,
        in_specs=placed,
        out_specs=P("aux", "orb", "ao"),
        check_vma=False,
    )
```

```python
import functools

import jax
import jax.numpy as jnp
from jax import lax
from jax.experimental import pallas as pl
from jax.experimental.pallas import tpu as pltpu
from jax.sharding import PartitionSpec as P

BF16 = jnp.bfloat16
F32 = jnp.float32
VMEM_LIMIT = 32 * 1024 * 1024
GROUPS = [[0, 1], [2, 3]]


def swap(x, axis, size, distance):
    return lax.ppermute(x, axis, [(i, i ^ distance) for i in range(size)])


def vmem():
    return pl.BlockSpec(memory_space=pltpu.VMEM)


def smem():
    return pl.BlockSpec(memory_space=pltpu.SMEM)


def stack_kernel(*refs):
    for j, part in enumerate(refs[:-1]):
        refs[-1][j] = part[...]


def behind(part, after):
    return lax.optimization_barrier((part, after))[0]


def left_kernel(orb_count, ao_count, slots, scalars, *refs):
    occ, (out, occ_all, upright) = refs[:ao_count], refs[ao_count:]
    block = occ[0].shape[1]
    rows = block // orb_count
    for t in range(ao_count):
        occ_all[t] = occ[t][...]
    orb = scalars[2 * slots]
    for s in range(orb_count):
        start = pl.multiple_of((orb ^ s) * rows, rows)
        for k in range(slots):
            live = (scalars[slots + k]).astype(F32).astype(BF16)
            to = (s * slots + k) * rows
            for j in range(orb_count):
                part = occ_all[scalars[k], j, pl.ds(start, rows), :]
                upright[to : to + rows, j * block : (j + 1) * block] = part * live
    out[...] = upright[...].T


def half_kernel(orb_count, left, *refs):
    raw, outs = refs[:orb_count], refs[orb_count:]
    slabs, slots, rows, width = raw[0].shape
    block = outs[0].shape[1]
    right = jnp.concatenate(
        [
            jnp.concatenate(
                [raw[s][p].reshape(slots * rows, width) for s in range(orb_count)], axis=0
            )
            for p in range(slabs)
        ],
        axis=1,
    )
    wide = jnp.dot(left[...], right, preferred_element_type=F32).astype(BF16)
    for j in range(orb_count):
        for p in range(slabs):
            outs[j][p] = wide[j * block : (j + 1) * block, p * width : (p + 1) * width]


def mask_kernel(per_shard, aux, domain, coeff, after, out, held, sem):
    copy = pltpu.make_async_copy(coeff, held, sem)
    copy.start()
    copy.wait()
    width = held.shape[1] // domain.shape[1]
    block = held.shape[0] // per_shard
    for b in range(per_shard):
        for c in range(domain.shape[1]):
            at = (slice(b * block, (b + 1) * block), slice(c * width, (c + 1) * width))
            mask = domain[aux[0] * per_shard + b, c].astype(F32).astype(BF16)
            out[at] = held[at] * mask


def virtual_kernel(aux_count, per_shard, aux, ao, *refs):
    shards, out = refs[:aux_count], refs[aux_count]
    block = out.shape[1]
    for s in range(aux_count):
        for b in range(per_shard):
            out[((aux[0] ^ s) * per_shard + b) ^ ao[0]] = shards[s][b * block : (b + 1) * block]


def final_kernel(ao_count, distances, orb, virtual, *refs):
    halves, (made, sems) = refs[: ao_count * len(distances)], refs[-2:]
    out = refs[-3] if refs[-3].ndim == 3 else refs[-4]
    slabs, rows, block = halves[0].shape
    right = virtual[...].reshape(ao_count * block, virtual.shape[2])
    copies = []
    for w, s in enumerate(distances):
        left = jnp.concatenate(
            [h[...].reshape(slabs * rows, block) for h in halves[w * ao_count : (w + 1) * ao_count]],
            axis=1,
        )
        wide = jnp.dot(left, right, preferred_element_type=F32)
        made[w] = wide.astype(made.dtype).reshape(made.shape[1:])
        start = pl.multiple_of((orb[0] ^ s) * slabs, slabs)
        copy = pltpu.make_async_copy(made.at[w], out.at[pl.ds(start, slabs)], sems.at[w])
        copy.start()
        copies.append(copy)
    for copy in copies:
        copy.wait()
    if refs[-3].ndim == 2:
        refs[-3][...] = jnp.zeros_like(refs[-3])


def gate_kernel(part, after, out):
    out[...] = part[...]


def gate(part, after):
    return pl.pallas_call(
        gate_kernel,
        out_shape=jax.ShapeDtypeStruct(part.shape, BF16),
        in_specs=[vmem(), pl.BlockSpec(memory_space=pl.ANY)],
        out_specs=vmem(),
        compiler_params=pltpu.CompilerParams(vmem_limit_bytes=VMEM_LIMIT),
    )(part, after)


def local(
    sizes, integrals, partner, pair_count, occupied_coeff, occupied_domain, virtual_coeff, virtual_domain
):
    aux_count, ao_count, orb_count = sizes
    chips = ao_count // 2
    aux, ao, orb = (lax.axis_index(name) for name in ("aux", "ao", "orb"))
    slab_rows, _, slots, rows, width = integrals.shape
    block = occupied_coeff.shape[0]
    share = slab_rows // orb_count
    order = [1, 2, 3, 0]
    raw_all = integrals.reshape(slab_rows, slots, rows, width)

    occ_own = occupied_coeff * occupied_domain[0, 0].astype(BF16)
    occ_by = {s: swap(occ_own, "orb", orb_count, s) if s else occ_own for s in order}
    occ_orb = [occ_by[s] for s in range(orb_count)]

    def raw_piece(s):
        return lax.dynamic_slice_in_dim(raw_all, (orb ^ s) * share, share, 0)

    raw_by = {s: swap(raw_piece(s), "orb", orb_count, s) if s else raw_piece(s) for s in [1, 2, 3, 0]}
    raw = [raw_by[s] for s in range(orb_count)]

    occ_stack = pl.pallas_call(
        stack_kernel,
        out_shape=jax.ShapeDtypeStruct((orb_count, block, block), BF16),
        in_specs=[vmem()] * orb_count,
        out_specs=vmem(),
        compiler_params=pltpu.CompilerParams(vmem_limit_bytes=VMEM_LIMIT),
    )(*occ_orb)
    occ_chip = [occ_stack] + [swap(occ_stack, "ao", ao_count, 2 * t) for t in range(1, chips)]
    occ = []
    for piece in occ_chip:
        occ += [piece, swap(piece, "ao", ao_count, 1)]

    scalars = jnp.concatenate(
        [
            partner[0] ^ ao,
            (jnp.arange(slots, dtype=jnp.int32) < pair_count[0]).astype(jnp.int32),
            orb.astype(jnp.int32)[None],
        ]
    )
    left = pl.pallas_call(
        functools.partial(left_kernel, orb_count, ao_count, slots),
        out_shape=jax.ShapeDtypeStruct((orb_count * block, slots * block), BF16),
        in_specs=[smem()] + [vmem()] * ao_count,
        out_specs=vmem(),
        scratch_shapes=[
            pltpu.VMEM((ao_count, orb_count, block, block), BF16),
            pltpu.VMEM((slots * block, orb_count * block), BF16),
        ],
        compiler_params=pltpu.CompilerParams(vmem_limit_bytes=VMEM_LIMIT),
    )(scalars, *occ)
    halves = pl.pallas_call(
        functools.partial(half_kernel, orb_count),
        out_shape=[jax.ShapeDtypeStruct((share, block, width), BF16)] * orb_count,
        in_specs=[vmem()] * (1 + orb_count),
        out_specs=[vmem()] * orb_count,
        compiler_params=pltpu.CompilerParams(vmem_limit_bytes=VMEM_LIMIT),
        cost_estimate=pl.CostEstimate(
            flops=2 * share * orb_count * orb_count * slots * rows * block * width,
            bytes_accessed=2 * 1024 * 1024,
            transcendentals=0,
        ),
    )(left, *raw)

    moved = {s: swap(halves[s], "orb", orb_count, s) if s else halves[s] for s in range(orb_count)}

    virtual_width = virtual_coeff.shape[1]
    per_shard = ao_count // aux_count
    aux_at, ao_at = (x.astype(jnp.int32)[None] for x in (aux, ao))
    masked = pl.pallas_call(
        functools.partial(mask_kernel, per_shard),
        out_shape=jax.ShapeDtypeStruct(virtual_coeff.shape, BF16),
        in_specs=[
            smem(),
            smem(),
            pl.BlockSpec(memory_space=pltpu.HBM),
            pl.BlockSpec(memory_space=pl.ANY),
        ],
        out_specs=vmem(),
        scratch_shapes=[pltpu.VMEM(virtual_coeff.shape, BF16), pltpu.SemaphoreType.DMA],
        compiler_params=pltpu.CompilerParams(vmem_limit_bytes=VMEM_LIMIT),
    )(aux_at, virtual_domain, virtual_coeff, occ_chip[-1])
    vir = [masked] + [swap(masked, "aux", aux_count, s) for s in range(1, aux_count)]
    virtual = pl.pallas_call(
        functools.partial(virtual_kernel, aux_count, per_shard),
        out_shape=jax.ShapeDtypeStruct((ao_count, block, virtual_width), BF16),
        in_specs=[smem()] * 2 + [vmem()] * aux_count,
        out_specs=vmem(),
        compiler_params=pltpu.CompilerParams(vmem_limit_bytes=VMEM_LIMIT),
        cost_estimate=pl.CostEstimate(
            flops=0,
            bytes_accessed=2*1024*1024,
            transcendentals=0,
        ),
    )(aux_at, ao_at, *vir)

    pieces = {}
    result, tokens = [], []

    def gather(s):
        mine = moved[s]
        last = s == orb_count - 1
        pieces[s] = []
        over = [mine] + [
            swap(mine, "ao", ao_count, 2 * t) for t in range(1, chips)
        ]
        for t, part in enumerate(over):
            sent = part
            if last and t > 0:
                sent = gate(part, tokens[0])
            pieces[s] += [part, swap(sent, "ao", ao_count, 1)]

    for distances in GROUPS:
        for s in distances:
            gather(s)
        taken = [part for s in distances for part in pieces[s]]
        made, *token = pl.pallas_call(
                functools.partial(final_kernel, ao_count, distances),
                out_shape=[
                    jax.ShapeDtypeStruct((slab_rows, block, virtual_width), BF16),
                ]
                + [jax.ShapeDtypeStruct((8, 128), F32)] * (distances != GROUPS[-1]),
                in_specs=[smem()] + [vmem()] * (1 + len(taken))
                + [pl.BlockSpec(memory_space=pl.ANY)] * len(result),
                out_specs=[pl.BlockSpec(memory_space=pl.ANY)]
                + [vmem()] * (distances != GROUPS[-1]),
                scratch_shapes=[
                    pltpu.VMEM((len(distances), share, block, virtual_width), BF16),
                    pltpu.SemaphoreType.DMA((len(distances),)),
                ],
                input_output_aliases={2 + len(taken): 0} if result else {},
                compiler_params=pltpu.CompilerParams(vmem_limit_bytes=VMEM_LIMIT),
                cost_estimate=pl.CostEstimate(
                    flops=2*1024*1024,
                    bytes_accessed=2*1024*1024,
                    transcendentals=0,
                ),
            )(orb.astype(jnp.int32)[None], virtual, *taken, *result)
        result = [made]
        tokens += token
    return result[0]


def solution(mesh):
    placed = (
        P("aux", "ao", None, "orb", None),
        P("ao", None),
        P("ao"),
        P("ao", "orb"),
        P("ao", "orb"),
        P("aux", "ao"),
        P(None, "ao"),
    )
    sizes = tuple(mesh.shape[name] for name in ("aux", "ao", "orb"))
    return jax.shard_map(
        functools.partial(local, sizes),
        mesh=mesh,
        in_specs=placed,
        out_specs=P("aux", "orb", "ao"),
        check_vma=False,
    )
```

```python
import functools

import jax
import jax.numpy as jnp
from jax import lax
from jax.experimental import pallas as pl
from jax.experimental.pallas import tpu as pltpu
from jax.sharding import PartitionSpec as P

BF16 = jnp.bfloat16
F32 = jnp.float32
VMEM_LIMIT = 32 * 1024 * 1024
GROUPS = [[0, 1], [2, 3]]


def swap(x, axis, size, distance):
    return lax.ppermute(x, axis, [(i, i ^ distance) for i in range(size)])


def vmem():
    return pl.BlockSpec(memory_space=pltpu.VMEM)


def smem():
    return pl.BlockSpec(memory_space=pltpu.SMEM)


def stack_kernel(*refs):
    for j, part in enumerate(refs[:-1]):
        refs[-1][j] = part[...]


def behind(part, after):
    return lax.optimization_barrier((part, after))[0]


def left_kernel(orb_count, ao_count, slots, scalars, *refs):
    occ, (out, occ_all, upright) = refs[:ao_count], refs[ao_count:]
    block = occ[0].shape[1]
    rows = block // orb_count
    for t in range(ao_count):
        occ_all[t] = occ[t][...]
    orb = scalars[2 * slots]
    for s in range(orb_count):
        start = pl.multiple_of((orb ^ s) * rows, rows)
        for k in range(slots):
            live = (scalars[slots + k]).astype(F32).astype(BF16)
            to = (s * slots + k) * rows
            for j in range(orb_count):
                part = occ_all[scalars[k], j, pl.ds(start, rows), :]
                upright[to : to + rows, j * block : (j + 1) * block] = part * live
    out[...] = upright[...].T


def half_kernel(orb_count, left, *refs):
    raw, outs = refs[:orb_count], refs[orb_count:]
    slabs, slots, rows, width = raw[0].shape
    block = outs[0].shape[1]
    right = jnp.concatenate(
        [
            jnp.concatenate(
                [raw[s][p].reshape(slots * rows, width) for s in range(orb_count)], axis=0
            )
            for p in range(slabs)
        ],
        axis=1,
    )
    wide = jnp.dot(left[...], right, preferred_element_type=F32).astype(BF16)
    for j in range(orb_count):
        for p in range(slabs):
            outs[j][p] = wide[j * block : (j + 1) * block, p * width : (p + 1) * width]


def mask_kernel(per_shard, aux, domain, coeff, after, out, held, sem):
    copy = pltpu.make_async_copy(coeff, held, sem)
    copy.start()
    copy.wait()
    width = held.shape[1] // domain.shape[1]
    block = held.shape[0] // per_shard
    for b in range(per_shard):
        for c in range(domain.shape[1]):
            at = (slice(b * block, (b + 1) * block), slice(c * width, (c + 1) * width))
            mask = domain[aux[0] * per_shard + b, c].astype(F32).astype(BF16)
            out[at] = held[at] * mask


def virtual_kernel(aux_count, per_shard, aux, ao, *refs):
    shards, out = refs[:aux_count], refs[aux_count]
    block = out.shape[1]
    for s in range(aux_count):
        for b in range(per_shard):
            out[((aux[0] ^ s) * per_shard + b) ^ ao[0]] = shards[s][b * block : (b + 1) * block]


def final_kernel(ao_count, distances, orb, virtual, *refs):
    halves, (made, sems) = refs[: ao_count * len(distances)], refs[-2:]
    out = refs[-3] if refs[-3].ndim == 3 else refs[-4]
    slabs, rows, block = halves[0].shape
    right = virtual[...].reshape(ao_count * block, virtual.shape[2])
    copies = []
    for w, s in enumerate(distances):
        left = jnp.concatenate(
            [h[...].reshape(slabs * rows, block) for h in halves[w * ao_count : (w + 1) * ao_count]],
            axis=1,
        )
        wide = jnp.dot(left, right, preferred_element_type=F32)
        made[w] = wide.astype(made.dtype).reshape(made.shape[1:])
        start = pl.multiple_of((orb[0] ^ s) * slabs, slabs)
        copy = pltpu.make_async_copy(made.at[w], out.at[pl.ds(start, slabs)], sems.at[w])
        copy.start()
        copies.append(copy)
    for copy in copies:
        copy.wait()
    if refs[-3].ndim == 2:
        refs[-3][...] = jnp.zeros_like(refs[-3])


def gate_kernel(part, after, out):
    out[...] = part[...]


def gate(part, after):
    return pl.pallas_call(
        gate_kernel,
        out_shape=jax.ShapeDtypeStruct(part.shape, BF16),
        in_specs=[vmem(), pl.BlockSpec(memory_space=pl.ANY)],
        out_specs=vmem(),
        compiler_params=pltpu.CompilerParams(vmem_limit_bytes=VMEM_LIMIT),
    )(part, after)


def local(
    sizes, integrals, partner, pair_count, occupied_coeff, occupied_domain, virtual_coeff, virtual_domain
):
    aux_count, ao_count, orb_count = sizes
    chips = ao_count // 2
    aux, ao, orb = (lax.axis_index(name) for name in ("aux", "ao", "orb"))
    slab_rows, _, slots, rows, width = integrals.shape
    block = occupied_coeff.shape[0]
    share = slab_rows // orb_count
    order = [1, 2, 3, 0]
    raw_all = integrals.reshape(slab_rows, slots, rows, width)

    occ_own = occupied_coeff * occupied_domain[0, 0].astype(BF16)
    occ_by = {s: swap(occ_own, "orb", orb_count, s) if s else occ_own for s in order}
    occ_orb = [occ_by[s] for s in range(orb_count)]

    def raw_piece(s):
        return lax.dynamic_slice_in_dim(raw_all, (orb ^ s) * share, share, 0)

    raw_by = {s: swap(raw_piece(s), "orb", orb_count, s) if s else raw_piece(s) for s in [1, 2, 3, 0]}
    raw = [raw_by[s] for s in range(orb_count)]

    occ_stack = pl.pallas_call(
        stack_kernel,
        out_shape=jax.ShapeDtypeStruct((orb_count, block, block), BF16),
        in_specs=[vmem()] * orb_count,
        out_specs=vmem(),
        compiler_params=pltpu.CompilerParams(vmem_limit_bytes=VMEM_LIMIT),
    )(*occ_orb)
    occ_chip = [occ_stack] + [swap(occ_stack, "ao", ao_count, 2 * t) for t in range(1, chips)]
    occ = []
    for piece in occ_chip:
        occ += [piece, swap(piece, "ao", ao_count, 1)]

    scalars = jnp.concatenate(
        [
            partner[0] ^ ao,
            (jnp.arange(slots, dtype=jnp.int32) < pair_count[0]).astype(jnp.int32),
            orb.astype(jnp.int32)[None],
        ]
    )
    left = pl.pallas_call(
        functools.partial(left_kernel, orb_count, ao_count, slots),
        out_shape=jax.ShapeDtypeStruct((orb_count * block, slots * block), BF16),
        in_specs=[smem()] + [vmem()] * ao_count,
        out_specs=vmem(),
        scratch_shapes=[
            pltpu.VMEM((ao_count, orb_count, block, block), BF16),
            pltpu.VMEM((slots * block, orb_count * block), BF16),
        ],
        compiler_params=pltpu.CompilerParams(vmem_limit_bytes=VMEM_LIMIT),
    )(scalars, *occ)
    halves = pl.pallas_call(
        functools.partial(half_kernel, orb_count),
        out_shape=[jax.ShapeDtypeStruct((share, block, width), BF16)] * orb_count,
        in_specs=[vmem()] * (1 + orb_count),
        out_specs=[vmem()] * orb_count,
        compiler_params=pltpu.CompilerParams(vmem_limit_bytes=VMEM_LIMIT),
        cost_estimate=pl.CostEstimate(
            flops=2 * share * orb_count * orb_count * slots * rows * block * width,
            bytes_accessed=2 * 1024 * 1024,
            transcendentals=0,
        ),
    )(left, *raw)

    moved = {s: swap(halves[s], "orb", orb_count, s) if s else halves[s] for s in range(orb_count)}

    virtual_width = virtual_coeff.shape[1]
    per_shard = ao_count // aux_count
    aux_at, ao_at = (x.astype(jnp.int32)[None] for x in (aux, ao))
    masked = pl.pallas_call(
        functools.partial(mask_kernel, per_shard),
        out_shape=jax.ShapeDtypeStruct(virtual_coeff.shape, BF16),
        in_specs=[
            smem(),
            smem(),
            pl.BlockSpec(memory_space=pltpu.HBM),
            pl.BlockSpec(memory_space=pl.ANY),
        ],
        out_specs=vmem(),
        scratch_shapes=[pltpu.VMEM(virtual_coeff.shape, BF16), pltpu.SemaphoreType.DMA],
        compiler_params=pltpu.CompilerParams(vmem_limit_bytes=VMEM_LIMIT),
    )(aux_at, virtual_domain, virtual_coeff, occ_stack)
    vir = [masked] + [swap(masked, "aux", aux_count, s) for s in range(1, aux_count)]
    virtual = pl.pallas_call(
        functools.partial(virtual_kernel, aux_count, per_shard),
        out_shape=jax.ShapeDtypeStruct((ao_count, block, virtual_width), BF16),
        in_specs=[smem()] * 2 + [vmem()] * aux_count,
        out_specs=vmem(),
        compiler_params=pltpu.CompilerParams(vmem_limit_bytes=VMEM_LIMIT),
        cost_estimate=pl.CostEstimate(
            flops=0,
            bytes_accessed=2*1024*1024,
            transcendentals=0,
        ),
    )(aux_at, ao_at, *vir)

    pieces = {}
    result, tokens = [], []

    def gather(s):
        mine = moved[s]
        last = s == orb_count - 1
        pieces[s] = []
        over = [mine] + [
            swap(mine, "ao", ao_count, 2 * t) for t in range(1, chips)
        ]
        for t, part in enumerate(over):
            sent = part
            if last and t > 0:
                sent = gate(part, tokens[0])
            pieces[s] += [part, swap(sent, "ao", ao_count, 1)]

    for distances in GROUPS:
        for s in distances:
            gather(s)
        taken = [part for s in distances for part in pieces[s]]
        made, *token = pl.pallas_call(
                functools.partial(final_kernel, ao_count, distances),
                out_shape=[
                    jax.ShapeDtypeStruct((slab_rows, block, virtual_width), BF16),
                ]
                + [jax.ShapeDtypeStruct((8, 128), F32)] * (distances != GROUPS[-1]),
                in_specs=[smem()] + [vmem()] * (1 + len(taken))
                + [pl.BlockSpec(memory_space=pl.ANY)] * len(result),
                out_specs=[pl.BlockSpec(memory_space=pl.ANY)]
                + [vmem()] * (distances != GROUPS[-1]),
                scratch_shapes=[
                    pltpu.VMEM((len(distances), share, block, virtual_width), BF16),
                    pltpu.SemaphoreType.DMA((len(distances),)),
                ],
                input_output_aliases={2 + len(taken): 0} if result else {},
                compiler_params=pltpu.CompilerParams(vmem_limit_bytes=VMEM_LIMIT),
                cost_estimate=pl.CostEstimate(
                    flops=2*1024*1024,
                    bytes_accessed=2*1024*1024,
                    transcendentals=0,
                ),
            )(orb.astype(jnp.int32)[None], virtual, *taken, *result)
        result = [made]
        tokens += token
    return result[0]


def solution(mesh):
    placed = (
        P("aux", "ao", None, "orb", None),
        P("ao", None),
        P("ao"),
        P("ao", "orb"),
        P("ao", "orb"),
        P("aux", "ao"),
        P(None, "ao"),
    )
    sizes = tuple(mesh.shape[name] for name in ("aux", "ao", "orb"))
    return jax.shard_map(
        functools.partial(local, sizes),
        mesh=mesh,
        in_specs=placed,
        out_specs=P("aux", "orb", "ao"),
        check_vma=False,
    )
```

```python
import functools

import jax
import jax.numpy as jnp
from jax import lax
from jax.experimental import pallas as pl
from jax.experimental.pallas import tpu as pltpu
from jax.sharding import PartitionSpec as P

BF16 = jnp.bfloat16
F32 = jnp.float32
VMEM_LIMIT = 32 * 1024 * 1024
GROUPS = [[0, 1], [2, 3]]


def swap(x, axis, size, distance):
    return lax.ppermute(x, axis, [(i, i ^ distance) for i in range(size)])


def vmem():
    return pl.BlockSpec(memory_space=pltpu.VMEM)


def smem():
    return pl.BlockSpec(memory_space=pltpu.SMEM)


def stack_kernel(*refs):
    for j, part in enumerate(refs[:-1]):
        refs[-1][j] = part[...]


def behind(part, after):
    return lax.optimization_barrier((part, after))[0]


def left_kernel(orb_count, ao_count, slots, scalars, *refs):
    occ, (out, occ_all, upright) = refs[:ao_count], refs[ao_count:]
    block = occ[0].shape[1]
    rows = block // orb_count
    for t in range(ao_count):
        occ_all[t] = occ[t][...]
    orb = scalars[2 * slots]
    for s in range(orb_count):
        start = pl.multiple_of((orb ^ s) * rows, rows)
        for k in range(slots):
            live = (scalars[slots + k]).astype(F32).astype(BF16)
            to = (s * slots + k) * rows
            for j in range(orb_count):
                part = occ_all[scalars[k], j, pl.ds(start, rows), :]
                upright[to : to + rows, j * block : (j + 1) * block] = part * live
    out[...] = upright[...].T


def half_kernel(orb_count, left, *refs):
    raw, outs = refs[:orb_count], refs[orb_count:]
    slabs, slots, rows, width = raw[0].shape
    block = outs[0].shape[1]
    right = jnp.concatenate(
        [
            jnp.concatenate(
                [raw[s][p].reshape(slots * rows, width) for s in range(orb_count)], axis=0
            )
            for p in range(slabs)
        ],
        axis=1,
    )
    wide = jnp.dot(left[...], right, preferred_element_type=F32).astype(BF16)
    for j in range(orb_count):
        for p in range(slabs):
            outs[j][p] = wide[j * block : (j + 1) * block, p * width : (p + 1) * width]


def mask_kernel(per_shard, aux, domain, coeff, after, out, held, sem):
    copy = pltpu.make_async_copy(coeff, held, sem)
    copy.start()
    copy.wait()
    width = held.shape[1] // domain.shape[1]
    block = held.shape[0] // per_shard
    for b in range(per_shard):
        for c in range(domain.shape[1]):
            at = (slice(b * block, (b + 1) * block), slice(c * width, (c + 1) * width))
            mask = domain[aux[0] * per_shard + b, c].astype(F32).astype(BF16)
            out[at] = held[at] * mask


def virtual_kernel(aux_count, per_shard, aux, ao, *refs):
    shards, out = refs[:aux_count], refs[aux_count]
    block = out.shape[1]
    for s in range(aux_count):
        for b in range(per_shard):
            out[((aux[0] ^ s) * per_shard + b) ^ ao[0]] = shards[s][b * block : (b + 1) * block]


def final_kernel(ao_count, distances, orb, virtual, *refs):
    halves, (made, sems) = refs[: ao_count * len(distances)], refs[-2:]
    out = refs[-3] if refs[-3].ndim == 3 else refs[-4]
    slabs, rows, block = halves[0].shape
    right = virtual[...].reshape(ao_count * block, virtual.shape[2])
    copies = []
    for w, s in enumerate(distances):
        left = jnp.concatenate(
            [h[...].reshape(slabs * rows, block) for h in halves[w * ao_count : (w + 1) * ao_count]],
            axis=1,
        )
        wide = jnp.dot(left, right, preferred_element_type=F32)
        made[w] = wide.astype(made.dtype).reshape(made.shape[1:])
        start = pl.multiple_of((orb[0] ^ s) * slabs, slabs)
        copy = pltpu.make_async_copy(made.at[w], out.at[pl.ds(start, slabs)], sems.at[w])
        copy.start()
        copies.append(copy)
    for copy in copies:
        copy.wait()
    if refs[-3].ndim == 2:
        refs[-3][...] = jnp.zeros_like(refs[-3])


def gate_kernel(part, after, out):
    out[...] = part[...]


def gate(part, after):
    return pl.pallas_call(
        gate_kernel,
        out_shape=jax.ShapeDtypeStruct(part.shape, BF16),
        in_specs=[vmem(), pl.BlockSpec(memory_space=pl.ANY)],
        out_specs=vmem(),
        compiler_params=pltpu.CompilerParams(vmem_limit_bytes=VMEM_LIMIT),
    )(part, after)


def local(
    sizes, integrals, partner, pair_count, occupied_coeff, occupied_domain, virtual_coeff, virtual_domain
):
    aux_count, ao_count, orb_count = sizes
    chips = ao_count // 2
    aux, ao, orb = (lax.axis_index(name) for name in ("aux", "ao", "orb"))
    slab_rows, _, slots, rows, width = integrals.shape
    block = occupied_coeff.shape[0]
    share = slab_rows // orb_count
    order = [1, 2, 3, 0]
    raw_all = integrals.reshape(slab_rows, slots, rows, width)

    occ_own = occupied_coeff * occupied_domain[0, 0].astype(BF16)
    occ_by = {s: swap(occ_own, "orb", orb_count, s) if s else occ_own for s in order}
    occ_orb = [occ_by[s] for s in range(orb_count)]

    def raw_piece(s):
        return lax.dynamic_slice_in_dim(raw_all, (orb ^ s) * share, share, 0)

    raw_by = {s: swap(raw_piece(s), "orb", orb_count, s) if s else raw_piece(s) for s in [1, 2, 3, 0]}
    raw = [raw_by[s] for s in range(orb_count)]

    occ_stack = pl.pallas_call(
        stack_kernel,
        out_shape=jax.ShapeDtypeStruct((orb_count, block, block), BF16),
        in_specs=[vmem()] * orb_count,
        out_specs=vmem(),
        compiler_params=pltpu.CompilerParams(vmem_limit_bytes=VMEM_LIMIT),
    )(*occ_orb)
    occ_chip = [occ_stack] + [swap(occ_stack, "ao", ao_count, 2 * t) for t in range(1, chips)]
    occ = []
    for piece in occ_chip:
        occ += [piece, swap(piece, "ao", ao_count, 1)]

    scalars = jnp.concatenate(
        [
            partner[0] ^ ao,
            (jnp.arange(slots, dtype=jnp.int32) < pair_count[0]).astype(jnp.int32),
            orb.astype(jnp.int32)[None],
        ]
    )
    left = pl.pallas_call(
        functools.partial(left_kernel, orb_count, ao_count, slots),
        out_shape=jax.ShapeDtypeStruct((orb_count * block, slots * block), BF16),
        in_specs=[smem()] + [vmem()] * ao_count,
        out_specs=vmem(),
        scratch_shapes=[
            pltpu.VMEM((ao_count, orb_count, block, block), BF16),
            pltpu.VMEM((slots * block, orb_count * block), BF16),
        ],
        compiler_params=pltpu.CompilerParams(vmem_limit_bytes=VMEM_LIMIT),
    )(scalars, *occ)
    halves = pl.pallas_call(
        functools.partial(half_kernel, orb_count),
        out_shape=[jax.ShapeDtypeStruct((share, block, width), BF16)] * orb_count,
        in_specs=[vmem()] * (1 + orb_count),
        out_specs=[vmem()] * orb_count,
        compiler_params=pltpu.CompilerParams(vmem_limit_bytes=VMEM_LIMIT),
        cost_estimate=pl.CostEstimate(
            flops=2 * share * orb_count * orb_count * slots * rows * block * width,
            bytes_accessed=2 * 1024 * 1024,
            transcendentals=0,
        ),
    )(left, *raw)

    moved = {s: swap(halves[s], "orb", orb_count, s) if s else halves[s] for s in range(orb_count)}

    virtual_width = virtual_coeff.shape[1]
    per_shard = ao_count // aux_count
    aux_at, ao_at = (x.astype(jnp.int32)[None] for x in (aux, ao))
    masked = pl.pallas_call(
        functools.partial(mask_kernel, per_shard),
        out_shape=jax.ShapeDtypeStruct(virtual_coeff.shape, BF16),
        in_specs=[
            smem(),
            smem(),
            pl.BlockSpec(memory_space=pltpu.HBM),
            pl.BlockSpec(memory_space=pl.ANY),
        ],
        out_specs=vmem(),
        scratch_shapes=[pltpu.VMEM(virtual_coeff.shape, BF16), pltpu.SemaphoreType.DMA],
        compiler_params=pltpu.CompilerParams(vmem_limit_bytes=VMEM_LIMIT),
    )(aux_at, virtual_domain, virtual_coeff, left)
    vir = [masked] + [swap(masked, "aux", aux_count, s) for s in range(1, aux_count)]
    virtual = pl.pallas_call(
        functools.partial(virtual_kernel, aux_count, per_shard),
        out_shape=jax.ShapeDtypeStruct((ao_count, block, virtual_width), BF16),
        in_specs=[smem()] * 2 + [vmem()] * aux_count,
        out_specs=vmem(),
        compiler_params=pltpu.CompilerParams(vmem_limit_bytes=VMEM_LIMIT),
        cost_estimate=pl.CostEstimate(
            flops=0,
            bytes_accessed=2*1024*1024,
            transcendentals=0,
        ),
    )(aux_at, ao_at, *vir)

    pieces = {}
    result, tokens = [], []

    def gather(s):
        mine = moved[s]
        last = s == orb_count - 1
        pieces[s] = []
        over = [mine] + [
            swap(mine, "ao", ao_count, 2 * t) for t in range(1, chips)
        ]
        for t, part in enumerate(over):
            sent = part
            if last and t > 0:
                sent = gate(part, tokens[0])
            pieces[s] += [part, swap(sent, "ao", ao_count, 1)]

    for distances in GROUPS:
        for s in distances:
            gather(s)
        taken = [part for s in distances for part in pieces[s]]
        made, *token = pl.pallas_call(
                functools.partial(final_kernel, ao_count, distances),
                out_shape=[
                    jax.ShapeDtypeStruct((slab_rows, block, virtual_width), BF16),
                ]
                + [jax.ShapeDtypeStruct((8, 128), F32)] * (distances != GROUPS[-1]),
                in_specs=[smem()] + [vmem()] * (1 + len(taken))
                + [pl.BlockSpec(memory_space=pl.ANY)] * len(result),
                out_specs=[pl.BlockSpec(memory_space=pl.ANY)]
                + [vmem()] * (distances != GROUPS[-1]),
                scratch_shapes=[
                    pltpu.VMEM((len(distances), share, block, virtual_width), BF16),
                    pltpu.SemaphoreType.DMA((len(distances),)),
                ],
                input_output_aliases={2 + len(taken): 0} if result else {},
                compiler_params=pltpu.CompilerParams(vmem_limit_bytes=VMEM_LIMIT),
                cost_estimate=pl.CostEstimate(
                    flops=2*1024*1024,
                    bytes_accessed=2*1024*1024,
                    transcendentals=0,
                ),
            )(orb.astype(jnp.int32)[None], virtual, *taken, *result)
        result = [made]
        tokens += token
    return result[0]


def solution(mesh):
    placed = (
        P("aux", "ao", None, "orb", None),
        P("ao", None),
        P("ao"),
        P("ao", "orb"),
        P("ao", "orb"),
        P("aux", "ao"),
        P(None, "ao"),
    )
    sizes = tuple(mesh.shape[name] for name in ("aux", "ao", "orb"))
    return jax.shard_map(
        functools.partial(local, sizes),
        mesh=mesh,
        in_specs=placed,
        out_specs=P("aux", "orb", "ao"),
        check_vma=False,
    )
```

```python
import functools

import jax
import jax.numpy as jnp
from jax import lax
from jax.experimental import pallas as pl
from jax.experimental.pallas import tpu as pltpu
from jax.sharding import PartitionSpec as P

BF16 = jnp.bfloat16
F32 = jnp.float32
VMEM_LIMIT = 32 * 1024 * 1024
GROUPS = [[0, 1], [2, 3]]


def swap(x, axis, size, distance):
    return lax.ppermute(x, axis, [(i, i ^ distance) for i in range(size)])


def vmem():
    return pl.BlockSpec(memory_space=pltpu.VMEM)


def smem():
    return pl.BlockSpec(memory_space=pltpu.SMEM)


def stack_kernel(*refs):
    for j, part in enumerate(refs[:-1]):
        refs[-1][j] = part[...]


def behind(part, after):
    return lax.optimization_barrier((part, after))[0]


def left_kernel(orb_count, ao_count, slots, scalars, *refs):
    occ, (out, occ_all, upright) = refs[:ao_count], refs[ao_count:]
    block = occ[0].shape[1]
    rows = block // orb_count
    for t in range(ao_count):
        occ_all[t] = occ[t][...]
    orb = scalars[2 * slots]
    for s in range(orb_count):
        start = pl.multiple_of((orb ^ s) * rows, rows)
        for k in range(slots):
            live = (scalars[slots + k]).astype(F32).astype(BF16)
            to = (s * slots + k) * rows
            for j in range(orb_count):
                part = occ_all[scalars[k], j, pl.ds(start, rows), :]
                upright[to : to + rows, j * block : (j + 1) * block] = part * live
    out[...] = upright[...].T


def half_kernel(orb_count, left, *refs):
    raw, outs = refs[:orb_count], refs[orb_count:]
    slabs, slots, rows, width = raw[0].shape
    block = outs[0].shape[1]
    right = jnp.concatenate(
        [
            jnp.concatenate(
                [raw[s][p].reshape(slots * rows, width) for s in range(orb_count)], axis=0
            )
            for p in range(slabs)
        ],
        axis=1,
    )
    wide = jnp.dot(left[...], right, preferred_element_type=F32).astype(BF16)
    for j in range(orb_count):
        for p in range(slabs):
            outs[j][p] = wide[j * block : (j + 1) * block, p * width : (p + 1) * width]


def mask_kernel(per_shard, aux, domain, coeff, after, out, held, sem):
    copy = pltpu.make_async_copy(coeff, held, sem)
    copy.start()
    copy.wait()
    width = held.shape[1] // domain.shape[1]
    block = held.shape[0] // per_shard
    for b in range(per_shard):
        for c in range(domain.shape[1]):
            at = (slice(b * block, (b + 1) * block), slice(c * width, (c + 1) * width))
            mask = domain[aux[0] * per_shard + b, c].astype(F32).astype(BF16)
            out[at] = held[at] * mask


def virtual_kernel(aux_count, per_shard, aux, ao, *refs):
    shards, out = refs[:aux_count], refs[aux_count]
    block = out.shape[1]
    for s in range(aux_count):
        for b in range(per_shard):
            out[((aux[0] ^ s) * per_shard + b) ^ ao[0]] = shards[s][b * block : (b + 1) * block]


def final_kernel(ao_count, distances, orb, virtual, *refs):
    halves, (made, sems) = refs[: ao_count * len(distances)], refs[-2:]
    out = refs[-3] if refs[-3].ndim == 3 else refs[-4]
    slabs, rows, block = halves[0].shape
    right = virtual[...].reshape(ao_count * block, virtual.shape[2])
    copies = []
    for w, s in enumerate(distances):
        left = jnp.concatenate(
            [h[...].reshape(slabs * rows, block) for h in halves[w * ao_count : (w + 1) * ao_count]],
            axis=1,
        )
        wide = jnp.dot(left, right, preferred_element_type=F32)
        made[w] = wide.astype(made.dtype).reshape(made.shape[1:])
        start = pl.multiple_of((orb[0] ^ s) * slabs, slabs)
        copy = pltpu.make_async_copy(made.at[w], out.at[pl.ds(start, slabs)], sems.at[w])
        copy.start()
        copies.append(copy)
    for copy in copies:
        copy.wait()
    if refs[-3].ndim == 2:
        refs[-3][...] = jnp.zeros_like(refs[-3])


def gate_kernel(part, after, out):
    out[...] = part[...]


def gate(part, after):
    return pl.pallas_call(
        gate_kernel,
        out_shape=jax.ShapeDtypeStruct(part.shape, BF16),
        in_specs=[vmem(), pl.BlockSpec(memory_space=pl.ANY)],
        out_specs=vmem(),
        compiler_params=pltpu.CompilerParams(vmem_limit_bytes=VMEM_LIMIT),
    )(part, after)


def local(
    sizes, integrals, partner, pair_count, occupied_coeff, occupied_domain, virtual_coeff, virtual_domain
):
    aux_count, ao_count, orb_count = sizes
    chips = ao_count // 2
    aux, ao, orb = (lax.axis_index(name) for name in ("aux", "ao", "orb"))
    slab_rows, _, slots, rows, width = integrals.shape
    block = occupied_coeff.shape[0]
    share = slab_rows // orb_count
    order = [1, 2, 3, 0]
    raw_all = integrals.reshape(slab_rows, slots, rows, width)

    occ_own = occupied_coeff * occupied_domain[0, 0].astype(BF16)
    occ_by = {s: swap(occ_own, "orb", orb_count, s) if s else occ_own for s in order}
    occ_orb = [occ_by[s] for s in range(orb_count)]

    def raw_piece(s):
        return lax.dynamic_slice_in_dim(raw_all, (orb ^ s) * share, share, 0)

    raw_by = {s: swap(raw_piece(s), "orb", orb_count, s) if s else raw_piece(s) for s in [1, 2, 3, 0]}
    raw = [raw_by[s] for s in range(orb_count)]

    occ_stack = pl.pallas_call(
        stack_kernel,
        out_shape=jax.ShapeDtypeStruct((orb_count, block, block), BF16),
        in_specs=[vmem()] * orb_count,
        out_specs=vmem(),
        compiler_params=pltpu.CompilerParams(vmem_limit_bytes=VMEM_LIMIT),
    )(*occ_orb)
    occ_chip = [occ_stack] + [swap(occ_stack, "ao", ao_count, 2 * t) for t in range(1, chips)]
    occ = []
    for piece in occ_chip:
        occ += [piece, swap(piece, "ao", ao_count, 1)]

    scalars = jnp.concatenate(
        [
            partner[0] ^ ao,
            (jnp.arange(slots, dtype=jnp.int32) < pair_count[0]).astype(jnp.int32),
            orb.astype(jnp.int32)[None],
        ]
    )
    left = pl.pallas_call(
        functools.partial(left_kernel, orb_count, ao_count, slots),
        out_shape=jax.ShapeDtypeStruct((orb_count * block, slots * block), BF16),
        in_specs=[smem()] + [vmem()] * ao_count,
        out_specs=vmem(),
        scratch_shapes=[
            pltpu.VMEM((ao_count, orb_count, block, block), BF16),
            pltpu.VMEM((slots * block, orb_count * block), BF16),
        ],
        compiler_params=pltpu.CompilerParams(vmem_limit_bytes=VMEM_LIMIT),
    )(scalars, *occ)
    halves = pl.pallas_call(
        functools.partial(half_kernel, orb_count),
        out_shape=[jax.ShapeDtypeStruct((share, block, width), BF16)] * orb_count,
        in_specs=[vmem()] * (1 + orb_count),
        out_specs=[vmem()] * orb_count,
        compiler_params=pltpu.CompilerParams(vmem_limit_bytes=VMEM_LIMIT),
        cost_estimate=pl.CostEstimate(
            flops=2 * share * orb_count * orb_count * slots * rows * block * width,
            bytes_accessed=2 * 1024 * 1024,
            transcendentals=0,
        ),
    )(left, *raw)

    moved = {s: swap(halves[s], "orb", orb_count, s) if s else halves[s] for s in range(orb_count)}

    virtual_width = virtual_coeff.shape[1]
    per_shard = ao_count // aux_count
    aux_at, ao_at = (x.astype(jnp.int32)[None] for x in (aux, ao))
    masked = pl.pallas_call(
        functools.partial(mask_kernel, per_shard),
        out_shape=jax.ShapeDtypeStruct(virtual_coeff.shape, BF16),
        in_specs=[
            smem(),
            smem(),
            pl.BlockSpec(memory_space=pltpu.HBM),
            pl.BlockSpec(memory_space=pl.ANY),
        ],
        out_specs=vmem(),
        scratch_shapes=[pltpu.VMEM(virtual_coeff.shape, BF16), pltpu.SemaphoreType.DMA],
        compiler_params=pltpu.CompilerParams(vmem_limit_bytes=VMEM_LIMIT),
    )(aux_at, virtual_domain, virtual_coeff, halves[0])
    vir = [masked] + [swap(masked, "aux", aux_count, s) for s in range(1, aux_count)]
    virtual = pl.pallas_call(
        functools.partial(virtual_kernel, aux_count, per_shard),
        out_shape=jax.ShapeDtypeStruct((ao_count, block, virtual_width), BF16),
        in_specs=[smem()] * 2 + [vmem()] * aux_count,
        out_specs=vmem(),
        compiler_params=pltpu.CompilerParams(vmem_limit_bytes=VMEM_LIMIT),
        cost_estimate=pl.CostEstimate(
            flops=0,
            bytes_accessed=2*1024*1024,
            transcendentals=0,
        ),
    )(aux_at, ao_at, *vir)

    pieces = {}
    result, tokens = [], []

    def gather(s):
        mine = moved[s]
        last = s == orb_count - 1
        pieces[s] = []
        over = [mine] + [
            swap(mine, "ao", ao_count, 2 * t) for t in range(1, chips)
        ]
        for t, part in enumerate(over):
            sent = part
            if last and t > 0:
                sent = gate(part, tokens[0])
            pieces[s] += [part, swap(sent, "ao", ao_count, 1)]

    for distances in GROUPS:
        for s in distances:
            gather(s)
        taken = [part for s in distances for part in pieces[s]]
        made, *token = pl.pallas_call(
                functools.partial(final_kernel, ao_count, distances),
                out_shape=[
                    jax.ShapeDtypeStruct((slab_rows, block, virtual_width), BF16),
                ]
                + [jax.ShapeDtypeStruct((8, 128), F32)] * (distances != GROUPS[-1]),
                in_specs=[smem()] + [vmem()] * (1 + len(taken))
                + [pl.BlockSpec(memory_space=pl.ANY)] * len(result),
                out_specs=[pl.BlockSpec(memory_space=pl.ANY)]
                + [vmem()] * (distances != GROUPS[-1]),
                scratch_shapes=[
                    pltpu.VMEM((len(distances), share, block, virtual_width), BF16),
                    pltpu.SemaphoreType.DMA((len(distances),)),
                ],
                input_output_aliases={2 + len(taken): 0} if result else {},
                compiler_params=pltpu.CompilerParams(vmem_limit_bytes=VMEM_LIMIT),
                cost_estimate=pl.CostEstimate(
                    flops=2*1024*1024,
                    bytes_accessed=2*1024*1024,
                    transcendentals=0,
                ),
            )(orb.astype(jnp.int32)[None], virtual, *taken, *result)
        result = [made]
        tokens += token
    return result[0]


def solution(mesh):
    placed = (
        P("aux", "ao", None, "orb", None),
        P("ao", None),
        P("ao"),
        P("ao", "orb"),
        P("ao", "orb"),
        P("aux", "ao"),
        P(None, "ao"),
    )
    sizes = tuple(mesh.shape[name] for name in ("aux", "ao", "orb"))
    return jax.shard_map(
        functools.partial(local, sizes),
        mesh=mesh,
        in_specs=placed,
        out_specs=P("aux", "orb", "ao"),
        check_vma=False,
    )
```
